256 devices in a mesh: row: 8 (over y, core), col: 32 (over x, z).
Axes of the slice: x: 4, y: 4, z: 8, core: 2. Of those that a mesh axis runs over, the one named last changes fastest.
Arguments:
- matrix: float32 [8, 8, 256, 2, 32, 256], P(None, 'row', None, None, 'col'), may hold values from -1.2 to 2.5, as said below
Outputs:
- factored: float32 [8, 8, 256, 2, 32, 256], P(None, 'row', None, None, 'col')
The draws below stay inside these ranges and needn't reach their ends.
Inputs may be any that keep to these rules, and one draw needn't show every extreme that they name: `matrix`: the leading 2 * 256 rows and columns, read from the lower triangle and mirrored, form a symmetric positive definite block.
All inputs are finite; a program needn't handle non-finite values.
Results may differ from the reference program's by a relative error of at most 0.00019.
Values sent between devices are 32-bit elements; how exact they have to be, the bound alone decides.
No kernel may reach another device: no remote copies, remote signals or barrier semaphores. Data moves between devices by JAX's collectives and lax.ppermute only.
A program may use at most 64 MiB of HBM per device.

```python
import jax
import jax.numpy as jnp
from jax import lax

NB = 256
TC = 2
TR = 8
N_ROW = 8
N_COL = 32


def squared_spread(points):
    leading = points.shape[0]
    total = jnp.zeros((leading, leading), jnp.float32)
    for group in range(16):
        piece = points[:, group * 16:(group + 1) * 16]
        spread = piece[:, None, :] - piece[None, :, :]
        total = total + jnp.sum(spread * spread, axis=2)
    return total


def draw_matrix(key, part):
    key = jax.random.fold_in(key, 7)
    key_bulk, key_points, key_jitter = jax.random.split(key, 3)
    matrix_order = TR * N_ROW * NB
    leading = 2 * NB
    background = jnp.clip(0.3 * jax.random.normal(key_bulk, (matrix_order, matrix_order), jnp.float32), -1.2, 1.2)
    points = jax.random.normal(key_points, (leading, 256), jnp.float32)
    jitter = jax.random.uniform(key_jitter, (leading,), jnp.float32, 0.5, 1.5)
    kernel = jnp.exp(-squared_spread(points) / 512.0)
    kernel = kernel + jnp.diag(jitter)
    whole_matrix = background.at[:leading, :leading].set(kernel)
    return whole_matrix.reshape(TR, N_ROW, NB, TC, N_COL, NB)


def setup_inputs(seed: int = 0) -> dict:
    key_of = jax.random.split(jax.random.key(seed), 2)
    return {
        "matrix": draw_matrix(jax.random.fold_in(key_of[1], 71), 0),
    }


def reference(matrix):
    matrix_order = TR * N_ROW * NB
    matrix_full = matrix.reshape(matrix_order, matrix_order)
    identity = jnp.eye(NB, dtype=jnp.float32)
    for step in range(2):
        start = step * NB
        finish = start + NB
        diag_tile = matrix_full[start:finish, start:finish]
        symmetric = jnp.tril(diag_tile) + jnp.tril(diag_tile, -1).T
        factor_tile = jnp.linalg.cholesky(symmetric)
        inverse = lax.linalg.triangular_solve(factor_tile, identity, left_side=True, lower=True)
        panel_block = jnp.dot(matrix_full[finish:, start:finish], inverse.T, precision=lax.Precision.HIGHEST)
        matrix_full = matrix_full.at[start:finish, start:finish].set(factor_tile)
        matrix_full = matrix_full.at[finish:, start:finish].set(panel_block)
        trailing = matrix_full[finish:, finish:]
        tile_index = jnp.arange(matrix_order - finish) // NB
        lower_tiles = tile_index[:, None] >= tile_index[None, :]
        product = jnp.dot(panel_block, panel_block.T, precision=lax.Precision.HIGHEST)
        trailing = jnp.where(lower_tiles, trailing - product, trailing)
        matrix_full = matrix_full.at[finish:, finish:].set(trailing)
    return matrix_full.reshape(matrix.shape)
```

```python
import jax
import jax.numpy as jnp
from jax import lax
from jax.experimental import pallas as pl
from jax.experimental.pallas import tpu as pltpu
from jax.sharding import PartitionSpec as P

F32 = jnp.float32
BF16 = jnp.bfloat16
N = 256
SLAB = 64
NY, NC, NX, NZ = 4, 2, 4, 8


def flat(y, c, x, z):
    return ((y * NC + c) * NX + x) * NZ + z


def pairs(fn):
    found = []
    for y in range(NY):
        for c in range(NC):
            for x in range(NX):
                for z in range(NZ):
                    to = fn(y, c, x, z)
                    if to is not None:
                        found.append((flat(y, c, x, z), flat(*to)))
    return found


def send(value, fn):
    return lax.ppermute(value, ("row", "col"), pairs(fn))


def sweep_slab(slab):
    left = [g[:, :128] for g in slab]
    right = [g[:, 128:] for g in slab]
    lane = lax.broadcasted_iota(jnp.int32, (8, 128), 1)
    sub = lax.broadcasted_iota(jnp.int32, (8, 128), 0)

    def splat(v):
        return jnp.broadcast_to(v, (8, 128))

    def assemble(rows):
        out = rows[0]
        for i in range(1, 8):
            out = jnp.where(sub == i, rows[i], out)
        return out

    z_left, z_right, u_left = [], [], []
    for s in range(len(slab)):
        a0, a1 = left[s], right[s]
        o = 8 * s
        cols = [splat(a0[:, o + j : o + j + 1]) for j in range(8)]
        d = [[splat(cols[j][i : i + 1, :]) for j in range(i + 1)] for i in range(8)]
        r0 = [splat(a0[i : i + 1, :]) for i in range(8)]
        r1 = [splat(a1[i : i + 1, :]) for i in range(8)]
        in_block = (lane >= o) & (lane < o + 8)
        r = []
        l = [[None] * 8 for _ in range(8)]
        zl, zr, ul = [], [], []
        for k in range(8):
            rk = lax.rsqrt(d[k][k])
            r.append(rk)
            for i in range(k + 1, 8):
                l[i][k] = d[i][k] * rk
            for j in range(k + 1, 8):
                for i in range(j, 8):
                    d[i][j] = d[i][j] - l[i][k] * l[j][k]
            x0 = jnp.where(in_block, jnp.where(lane == o + k, 1.0, 0.0).astype(F32), r0[k])
            x1 = r1[k]
            x2 = r0[k]
            for m in range(k):
                x0 = x0 - l[k][m] * zl[m]
                x1 = x1 - l[k][m] * zr[m]
                x2 = x2 - l[k][m] * ul[m]
            zl.append(x0 * rk)
            zr.append(x1 * rk)
            ul.append(x2 * rk)
        z_left.append(assemble(zl))
        z_right.append(assemble(zr))
        u_left.append(assemble(ul))
        for t in range(s + 1, len(slab)):
            coef = []
            for k in range(8):
                c = splat(left[t][:, o + k : o + k + 1])
                for m in range(k):
                    c = c - l[k][m] * coef[m]
                coef.append(c * r[k])
            x0 = jnp.where(in_block, 0.0, left[t])
            x1 = right[t]
            for k in range(8):
                x0 = x0 - coef[k] * zl[k]
                x1 = x1 - coef[k] * zr[k]
            left[t] = x0
            right[t] = x1
    return z_left, z_right, u_left


def factor_tile(m_ref, u_ref):
    row = lax.broadcasted_iota(jnp.int32, (N, N), 0)
    lan = lax.broadcasted_iota(jnp.int32, (N, N), 1)
    row_s = lax.broadcasted_iota(jnp.int32, (SLAB, N), 0)
    lan_s = lax.broadcasted_iota(jnp.int32, (SLAB, N), 1)

    @pl.loop(0, N // SLAB)
    def _(b):
        o = b * SLAB
        rows = pl.ds(pl.multiple_of(o, SLAB), SLAB)
        slab = pltpu.roll(m_ref[rows, :], N - o, 1)
        zl, zr, ul = sweep_slab([slab[8 * g : 8 * g + 8, :] for g in range(SLAB // 8)])
        zr = jnp.concatenate(zr, 0)
        z = jnp.concatenate([jnp.concatenate(zl, 0), zr], 1)
        u = jnp.concatenate([jnp.concatenate(ul, 0), zr], 1)
        z = jnp.where((lan_s < SLAB) & (lan_s > row_s), 0.0, z)
        z = pltpu.roll(z, o, 1)
        u = pltpu.roll(u, o, 1)
        u_ref[rows, :] = u

        @pl.when(b < N // SLAB - 1)
        def _():
            coef = jnp.where(lan_s >= o + SLAB, u, 0.0)
            update = lax.dot_general(
                coef, z, (((0,), (0,)), ((), ())), precision=lax.Precision.HIGHEST, preferred_element_type=F32
            )
            m = m_ref[...]
            m = jnp.where((row >= o + SLAB) & (lan >= o) & (lan < o + SLAB), 0.0, m)
            m_ref[...] = m - update

        m_ref[rows, :] = z


def dot_nt(a, b):
    return lax.dot_general(a, b, (((1,), (1,)), ((), ())), precision=lax.Precision.HIGHEST, preferred_element_type=F32)


def factor_kernel(packed_ref, a10_ref, l0_ref, w0_ref, p10_ref, l1_ref, w1_ref, m_ref, u_ref):
    row = lax.broadcasted_iota(jnp.int32, (N, N), 0)
    lan = lax.broadcasted_iota(jnp.int32, (N, N), 1)

    def read_out(l_ref, w_ref):
        l_ref[...] = jnp.where(row >= lan, u_ref[...].T, 0.0)
        w_ref[...] = jnp.where(row >= lan, m_ref[...], 0.0)

    packed = packed_ref[:N, :]
    turned = packed.T
    m_ref[...] = jnp.where(row >= lan, packed, turned)
    factor_tile(m_ref, u_ref)
    read_out(l0_ref, w0_ref)
    p10 = dot_nt(a10_ref[:N, :], w0_ref[...])
    p10_ref[...] = p10
    packed = packed_ref[:N, :]
    diag = jnp.broadcast_to(packed_ref[N : N + 1, :], (N, N))
    second = jnp.where(row == lan, diag, jnp.where(row < lan, packed, packed.T))
    m_ref[...] = second - dot_nt(p10, p10)
    factor_tile(m_ref, u_ref)
    read_out(l1_ref, w1_ref)


def factor(packed, a10):
    return pl.pallas_call(
        factor_kernel,
        out_shape=[jax.ShapeDtypeStruct((N, N), F32)] * 5,
        in_specs=[pl.BlockSpec(memory_space=pltpu.VMEM)] * 2,
        out_specs=[pl.BlockSpec(memory_space=pltpu.VMEM)] * 5,
        scratch_shapes=[pltpu.VMEM((N, N), F32)] * 2,
        compiler_params=pltpu.CompilerParams(vmem_limit_bytes=24 << 20),
        cost_estimate=pl.CostEstimate(flops=10**9, bytes_accessed=60 << 20, transcendentals=0),
        name="factor",
    )(packed, a10)


def order_kernel(z_ref, *refs):
    pieces, out_ref, sem = refs[:NZ], refs[NZ], refs[NZ + 1]
    z = z_ref[0]
    copies = []
    for d in range(NZ):
        slot = lax.rem(z + (NZ - d), NZ)
        for c in range(2):
            copies.append(
                pltpu.make_async_copy(
                    pieces[d].at[c],
                    out_ref.at[pl.ds(pl.multiple_of(slot * 64, 64), 64), pl.ds(c * N, N)],
                    sem.at[d, c],
                )
            )
    for copy in copies:
        copy.start()
    for copy in copies:
        copy.wait()


def order(z, pieces):
    return pl.pallas_call(
        order_kernel,
        out_shape=jax.ShapeDtypeStruct((2 * N, 2 * N), F32),
        in_specs=[pl.BlockSpec(memory_space=pltpu.SMEM)] + [pl.BlockSpec(memory_space=pl.ANY)] * NZ,
        out_specs=pl.BlockSpec(memory_space=pl.ANY),
        scratch_shapes=[pltpu.SemaphoreType.DMA((NZ, 2))],
        cost_estimate=pl.CostEstimate(flops=0, bytes_accessed=2 << 20, transcendentals=0),
        name="order",
    )(z, *pieces)


def split(v):
    hi = v.astype(BF16)
    return hi, (v - hi.astype(F32)).astype(BF16)


def update_kernel(
    amap_ref, info_ref, m_ref, q0, q1, q2, q3, own_ref, other_ref, l0_ref, w0_ref, p10_ref, l1_ref, w1_ref,
    o_ref, w0t, w1t, p10t, x_s, chi, clo, p_s,
):
    t = pl.program_id(0)
    p, q, keep_own = info_ref[0], info_ref[1], info_ref[2]
    a = amap_ref[t]
    i = a * 8 + p

    def dot_hi(u, v):
        return jnp.dot(u, v, precision=lax.Precision.HIGHEST, preferred_element_type=F32)

    def solve(x):
        first = dot_hi(x[:, :N], w0t[...])
        rest = x[:, N:] - dot_hi(first, p10t[...])
        return first, dot_hi(rest, w1t[...])

    @pl.when(t == 0)
    def _():
        w0t[...] = w0_ref[...].T
        w1t[...] = w1_ref[...].T
        p10t[...] = p10_ref[...].T
        for b in range(2):
            rows = pl.ds(b * N, N)

            @pl.when(keep_own == 1)
            def _():
                x_s[...] = own_ref[rows, :]

            @pl.when(keep_own == 0)
            def _():
                x_s[...] = other_ref[rows, :]

            for k, panel in enumerate(solve(x_s[...])):
                hi, lo = split(panel.T)
                chi[pl.ds(k * N, N), pl.ds(b * N, N)] = hi
                clo[pl.ds(k * N, N), pl.ds(b * N, N)] = lo

    for d, ref in enumerate((q0, q1, q2, q3)):
        @pl.when(t // 2 == d)
        def _(ref=ref):
            x_s[...] = ref[...]

    first, second = solve(x_s[...])
    p_s[:, :N] = first
    p_s[:, N:] = second

    def put(b, value):
        for half in range(2):
            o_ref[pl.ds(2 * b + half, N, stride=4), :] = value[:, half * 128 : half * 128 + 128]

    def get(b):
        return jnp.concatenate([m_ref[pl.ds(2 * b + half, N, stride=4), :] for half in range(2)], 1)

    for b in range(2):
        j = 32 * b + q
        is_first = j == 0
        is_second = j == 1
        updates = (j > 1) & (i >= j)

        @pl.when(updates)
        def _(b=b):
            phi, plo = split(p_s[...])
            cols = pl.ds(b * N, N)
            chi_b, clo_b = chi[:, cols], clo[:, cols]

            def dot16(u, v):
                return jnp.dot(u, v, preferred_element_type=F32)

            product = dot16(plo, chi_b) + dot16(phi, clo_b) + dot16(phi, chi_b)
            put(b, get(b) - product)

        @pl.when((j > 1) & (i < j) | is_second & (i < 1))
        def _(b=b):
            put(b, get(b))

        if b == 0:
            @pl.when(is_first & (i == 0))
            def _():
                put(0, l0_ref[...])

            @pl.when(is_first & (i > 0))
            def _():
                put(0, p_s[:, :N])

            @pl.when(is_second & (i == 1))
            def _():
                put(0, l1_ref[...])

            @pl.when(is_second & (i > 1))
            def _():
                put(0, p_s[:, N:])


def update(amap, info, flat_blocks, quarters, own, other, l0, w0, p10, l1, w1):
    whole = lambda shape: pl.BlockSpec(shape, lambda t, amap, info: (0, 0))
    quarter = lambda d: pl.BlockSpec((N, 2 * N), lambda t, amap, info: (jnp.clip(t - 2 * d, 0, 1), 0))
    tiles = pl.BlockSpec((4 * N, 128), lambda t, amap, info: (amap[t], 0))
    return pl.pallas_call(
        update_kernel,
        grid_spec=pltpu.PrefetchScalarGridSpec(
            num_scalar_prefetch=2,
            grid=(8,),
            in_specs=[tiles] + [quarter(d) for d in range(4)] + [whole((2 * N, 2 * N))] * 2 + [whole((N, N))] * 5,
            out_specs=tiles,
            scratch_shapes=[pltpu.VMEM((N, N), F32)] * 3
            + [pltpu.VMEM((N, 2 * N), F32)]
            + [pltpu.VMEM((2 * N, 2 * N), BF16)] * 2
            + [pltpu.VMEM((N, 2 * N), F32)],
        ),
        out_shape=jax.ShapeDtypeStruct(flat_blocks.shape, F32),
        compiler_params=pltpu.CompilerParams(vmem_limit_bytes=48 << 20, dimension_semantics=("arbitrary",)),
        cost_estimate=pl.CostEstimate(flops=6 * 10**9, bytes_accessed=16 << 20, transcendentals=0),
        name="update",
    )(amap, info, flat_blocks, *quarters, own, other, l0, w0, p10, l1, w1)


def on_device(matrix):
    row_index = lax.axis_index("row")
    col_index = lax.axis_index("col")
    y, core = row_index // NC, row_index % NC
    x, z = col_index // NZ, col_index % NZ
    blocks = matrix.reshape(8, N, 2, N)
    flat_blocks = matrix.reshape(8 * N * 4, 128)
    column = blocks[:, :, 0, :]

    tile = column[0]
    second = send(tile, lambda y, c, x, z: (0, 0, 0, 0) if (y, c, x, z) == (0, 1, 0, 1) else None)
    lower = jnp.tril(tile) + jnp.triu(second.T, 1)
    extra = jnp.concatenate([jnp.diagonal(second)[None, :], jnp.zeros((7, N), F32)], 0)
    item = jnp.where(core == 0, jnp.concatenate([lower, extra], 0), jnp.concatenate([tile, jnp.zeros((8, N), F32)], 0))

    arrived = [
        send(column[d::4], lambda y, c, x, z, d=d: (y, c, d, z) if x == 0 and z < 2 else None) for d in (1, 2, 3)
    ]

    def spread(item, mine, ops):
        got = [send(item, fn) for fn in ops]
        out = jnp.where(mine, item, 0.0)
        for g in got:
            out = out + g
        return out

    item = spread(
        item, (y == 0) & (x == 0) & (z == 0),
        [lambda y, c, x, z, d=d: (d, c, 0, 0) if (y, x, z) == (0, 0, 0) else None for d in (1, 2, 3)],
    )
    item = spread(
        item, (x == 0) & (z == 0),
        [lambda y, c, x, z, d=d: (y, c, 0, d) if (x, z) == (0, 0) else None for d in (2, 4, 6)],
    )
    item = spread(
        item, (x == 0) & (z % 2 == 0),
        [lambda y, c, x, z: (y, c, 0, z + 1) if x == 0 and z % 2 == 0 else None],
    )
    item = spread(
        item, x == 0,
        [lambda y, c, x, z, d=d: (y, c, d, z) if x == 0 else None for d in (1, 2, 3)],
    )
    swapped = send(item, lambda y, c, x, z: (y, 1 - c, x, z))

    quarter = jnp.where((x == 0) & (z < 2), column[0::4], 0.0) + arrived[0] + arrived[1] + arrived[2]
    parts = quarter.reshape(NZ, 64, N)
    landed = [lax.dynamic_index_in_dim(parts, z, 0, keepdims=False)]
    for d in range(1, NZ):
        part = lax.dynamic_index_in_dim(parts, (z + d) % NZ, 0, keepdims=False)
        landed.append(send(part, lambda y, c, x, z, d=d: (y, c, x, (z + d) % NZ) if z < 2 else None))
    landed = jnp.stack(landed)
    piece = jnp.stack(
        [
            lax.dynamic_index_in_dim(landed, z, 0, keepdims=False),
            lax.dynamic_index_in_dim(landed, (z + NZ - 1) % NZ, 0, keepdims=False),
        ]
    )

    pieces = [piece] + [send(piece, lambda y, c, x, z, d=d: (y, c, x, (z + d) % NZ)) for d in range(1, NZ)]
    mine = order(z.astype(jnp.int32)[None], pieces)
    quarters = [mine] + [send(mine, lambda y, c, x, z, d=d: (y, c, (x + d) % NX, z)) for d in (1, 2, 3)]

    chosen = [
        send(mine, lambda y, c, x, z, d=d: ((y + d) % NY, c, x, z) if y * NC + c == z else None) for d in (1, 2, 3)
    ]
    own = jnp.where(row_index == z, mine, 0.0) + chosen[0] + chosen[1] + chosen[2]
    other = send(own, lambda y, c, x, z: (y, 1 - c, x, z))

    packed, a10 = jnp.where(core == 0, item, swapped), jnp.where(core == 0, swapped, item)
    packed, a10, _ = lax.optimization_barrier((packed, a10, mine))
    l0, w0, p10, l1, w1 = factor(packed, a10)

    steps = jnp.arange(8, dtype=jnp.int32)
    amap = (x.astype(jnp.int32) - steps // 2 + NX) % NX + 4 * (steps % 2)
    info = jnp.stack([row_index, col_index, (core == z % 2).astype(jnp.int32)]).astype(jnp.int32)
    out = update(amap, info, flat_blocks, quarters, own, other, l0, w0, p10, l1, w1)
    return out.reshape(matrix.shape)


def solution(mesh):
    return jax.shard_map(
        on_device,
        mesh=mesh,
        in_specs=(P(None, "row", None, None, "col", None),),
        out_specs=P(None, "row", None, None, "col", None),
        check_vma=False,
    )
```

```python
import jax
import jax.numpy as jnp
from jax import lax
from jax.experimental import pallas as pl
from jax.experimental.pallas import tpu as pltpu
from jax.sharding import PartitionSpec as P

F32 = jnp.float32
BF16 = jnp.bfloat16
N = 256
SLAB = 64
NY, NC, NX, NZ = 4, 2, 4, 8


def flat(y, c, x, z):
    return ((y * NC + c) * NX + x) * NZ + z


def pairs(fn):
    found = []
    for y in range(NY):
        for c in range(NC):
            for x in range(NX):
                for z in range(NZ):
                    to = fn(y, c, x, z)
                    if to is not None:
                        found.append((flat(y, c, x, z), flat(*to)))
    return found


def send(value, fn):
    return lax.ppermute(value, ("row", "col"), pairs(fn))


def sweep_slab(slab):
    left = [g[:, :128] for g in slab]
    right = [g[:, 128:] for g in slab]
    lane = lax.broadcasted_iota(jnp.int32, (8, 128), 1)
    sub = lax.broadcasted_iota(jnp.int32, (8, 128), 0)

    def splat(v):
        return jnp.broadcast_to(v, (8, 128))

    def assemble(rows):
        out = rows[0]
        for i in range(1, 8):
            out = jnp.where(sub == i, rows[i], out)
        return out

    z_left, z_right, u_left = [], [], []
    for s in range(len(slab)):
        a0, a1 = left[s], right[s]
        o = 8 * s
        cols = [splat(a0[:, o + j : o + j + 1]) for j in range(8)]
        d = [[splat(cols[j][i : i + 1, :]) for j in range(i + 1)] for i in range(8)]
        r0 = [splat(a0[i : i + 1, :]) for i in range(8)]
        r1 = [splat(a1[i : i + 1, :]) for i in range(8)]
        in_block = (lane >= o) & (lane < o + 8)
        r = []
        l = [[None] * 8 for _ in range(8)]
        zl, zr, ul = [], [], []
        for k in range(8):
            rk = lax.rsqrt(d[k][k])
            r.append(rk)
            for i in range(k + 1, 8):
                l[i][k] = d[i][k] * rk
            for j in range(k + 1, 8):
                for i in range(j, 8):
                    d[i][j] = d[i][j] - l[i][k] * l[j][k]
            x0 = jnp.where(in_block, jnp.where(lane == o + k, 1.0, 0.0).astype(F32), r0[k])
            x1 = r1[k]
            x2 = r0[k]
            for m in range(k):
                x0 = x0 - l[k][m] * zl[m]
                x1 = x1 - l[k][m] * zr[m]
                x2 = x2 - l[k][m] * ul[m]
            zl.append(x0 * rk)
            zr.append(x1 * rk)
            ul.append(x2 * rk)
        z_left.append(assemble(zl))
        z_right.append(assemble(zr))
        u_left.append(assemble(ul))
        for t in range(s + 1, len(slab)):
            coef = []
            for k in range(8):
                c = splat(left[t][:, o + k : o + k + 1])
                for m in range(k):
                    c = c - l[k][m] * coef[m]
                coef.append(c * r[k])
            x0 = jnp.where(in_block, 0.0, left[t])
            x1 = right[t]
            for k in range(8):
                x0 = x0 - coef[k] * zl[k]
                x1 = x1 - coef[k] * zr[k]
            left[t] = x0
            right[t] = x1
    return z_left, z_right, u_left


def factor_tile(m_ref, u_ref):
    row = lax.broadcasted_iota(jnp.int32, (N, N), 0)
    lan = lax.broadcasted_iota(jnp.int32, (N, N), 1)
    row_s = lax.broadcasted_iota(jnp.int32, (SLAB, N), 0)
    lan_s = lax.broadcasted_iota(jnp.int32, (SLAB, N), 1)

    @pl.loop(0, N // SLAB)
    def _(b):
        o = b * SLAB
        rows = pl.ds(pl.multiple_of(o, SLAB), SLAB)
        slab = pltpu.roll(m_ref[rows, :], N - o, 1)
        zl, zr, ul = sweep_slab([slab[8 * g : 8 * g + 8, :] for g in range(SLAB // 8)])
        zr = jnp.concatenate(zr, 0)
        z = jnp.concatenate([jnp.concatenate(zl, 0), zr], 1)
        u = jnp.concatenate([jnp.concatenate(ul, 0), zr], 1)
        z = jnp.where((lan_s < SLAB) & (lan_s > row_s), 0.0, z)
        z = pltpu.roll(z, o, 1)
        u = pltpu.roll(u, o, 1)
        u_ref[rows, :] = u

        @pl.when(b < N // SLAB - 1)
        def _():
            coef = jnp.where(lan_s >= o + SLAB, u, 0.0)
            update = lax.dot_general(
                coef, z, (((0,), (0,)), ((), ())), precision=lax.Precision.HIGHEST, preferred_element_type=F32
            )
            m = m_ref[...]
            m = jnp.where((row >= o + SLAB) & (lan >= o) & (lan < o + SLAB), 0.0, m)
            m_ref[...] = m - update

        m_ref[rows, :] = z


def dot_nt(a, b):
    return lax.dot_general(a, b, (((1,), (1,)), ((), ())), precision=lax.Precision.HIGHEST, preferred_element_type=F32)


def read_out(l_ref, w_ref, m_ref, u_ref):
    row = lax.broadcasted_iota(jnp.int32, (N, N), 0)
    lan = lax.broadcasted_iota(jnp.int32, (N, N), 1)
    l_ref[...] = jnp.where(row >= lan, u_ref[...].T, 0.0)
    w_ref[...] = jnp.where(row >= lan, m_ref[...], 0.0)


def factor_kernel(core_ref, own_ref, other_ref, l0_ref, w0_ref, p10_ref, l1_ref, w1_ref, m_ref, u_ref):
    row = lax.broadcasted_iota(jnp.int32, (N, N), 0)
    lan = lax.broadcasted_iota(jnp.int32, (N, N), 1)

    def half(core, lo, hi):
        return jnp.where(core_ref[0] == core, own_ref[:, lo:hi, :], other_ref[:, lo:hi, :])

    def mirrored(core):
        t = half(core, 0, 8).reshape(N, N)
        return jnp.where(row >= lan, t, t.T)

    m_ref[...] = mirrored(0)
    factor_tile(m_ref, u_ref)
    read_out(l0_ref, w0_ref, m_ref, u_ref)
    a10 = jnp.concatenate([half(0, 8, 12), half(1, 8, 12)], 1).reshape(N, N)
    p10 = dot_nt(a10, w0_ref[...])
    p10_ref[...] = p10
    m_ref[...] = mirrored(1) - dot_nt(p10, p10)
    factor_tile(m_ref, u_ref)
    read_out(l1_ref, w1_ref, m_ref, u_ref)


def factor(core, own, other):
    vmem = pl.BlockSpec(memory_space=pltpu.VMEM)
    return pl.pallas_call(
        factor_kernel,
        out_shape=[jax.ShapeDtypeStruct((N, N), F32)] * 5,
        in_specs=[pl.BlockSpec(memory_space=pltpu.SMEM), vmem, vmem],
        out_specs=[vmem] * 5,
        scratch_shapes=[pltpu.VMEM((N, N), F32)] * 2,
        compiler_params=pltpu.CompilerParams(vmem_limit_bytes=24 << 20),
        cost_estimate=pl.CostEstimate(flops=10**9, bytes_accessed=60 << 20, transcendentals=0),
        name="factor",
    )(core, own, other)


def column_kernel(m_ref, o_ref):
    for half in range(2):
        o_ref[0, 0, :, half * 128 : half * 128 + 128] = m_ref[pl.ds(half, N, stride=4), :]


def first_column(flat_blocks):
    return pl.pallas_call(
        column_kernel,
        grid=(8,),
        out_shape=jax.ShapeDtypeStruct((4, 2, N, N), F32),
        in_specs=[pl.BlockSpec((4 * N, 128), lambda a: (a, 0))],
        out_specs=pl.BlockSpec((1, 1, N, N), lambda a: (a % 4, a // 4, 0, 0)),
        compiler_params=pltpu.CompilerParams(vmem_limit_bytes=16 << 20, dimension_semantics=("arbitrary",)),
        cost_estimate=pl.CostEstimate(flops=0, bytes_accessed=6 << 20, transcendentals=0),
        name="first_column",
    )(flat_blocks)


def split(v):
    hi = v.astype(BF16)
    return hi, (v - hi.astype(F32)).astype(BF16)


def dot_nn(a, b):
    return jnp.dot(a, b, precision=lax.Precision.HIGHEST, preferred_element_type=F32)


def rows_kernel(info_ref, w0_ref, p10_ref, w1_ref, a0, a1, a2, a3, b0, b1, b2, b3, o_ref):
    t = pl.program_id(0)
    odd = info_ref[3]
    for d, (mine, others) in enumerate(((a0, b0), (a1, b1), (a2, b2), (a3, b3))):
        @pl.when(t == d)
        def _(mine=mine, others=others):
            even = odd == 0
            x0 = jnp.where(even, mine[...], others[...])
            x1 = jnp.where(even, others[...], mine[...])
            first = dot_nt(x0, w0_ref[...])
            o_ref[0, :, :N] = first
            o_ref[0, :, N:] = dot_nt(x1 - dot_nt(first, p10_ref[...]), w1_ref[...])


def solve_rows(info, w0, p10, w1, own_quarters, other_quarters):
    whole = lambda *shape: pl.BlockSpec(shape, lambda t: (0,) * len(shape))
    return pl.pallas_call(
        rows_kernel,
        grid=(4,),
        in_specs=[pl.BlockSpec(memory_space=pltpu.SMEM)] + [whole(N, N)] * 3 + [whole(2 * N, N)] * 8,
        out_specs=pl.BlockSpec((1, 2 * N, 2 * N), lambda t: (t, 0, 0)),
        out_shape=jax.ShapeDtypeStruct((4, 2 * N, 2 * N), F32),
        compiler_params=pltpu.CompilerParams(vmem_limit_bytes=60 << 20, dimension_semantics=("arbitrary",)),
        cost_estimate=pl.CostEstimate(flops=5 * 10**9, bytes_accessed=9 << 20, transcendentals=0),
        name="solve_rows",
    )(info, w0, p10, w1, *own_quarters, *other_quarters)


def update_kernel(
    info_ref, m_ref, p_ref, own_ref, other_ref, l0_ref, w0_ref, p10_ref, l1_ref, w1_ref, o_ref, x_s, chi, clo
):
    t = pl.program_id(0)
    p, q, keep_own, x = info_ref[0], info_ref[1], info_ref[2], info_ref[4]
    i = 8 * lax.rem(x - t + 4, 4) + p

    @pl.when(t == 0)
    def _():
        for value, kept in ((own_ref, 1), (other_ref, 0)):
            @pl.when(keep_own == kept)
            def _(value=value):
                x_s[...] = value[...]

        first = dot_nt(w0_ref[...], x_s[0])
        second = dot_nn(w1_ref[...], x_s[1].T - dot_nn(p10_ref[...], first))
        for k, panel in enumerate((first, second)):
            hi, lo = split(panel)
            chi[k * N : k * N + N, :] = hi
            clo[k * N : k * N + N, :] = lo

    def put(h, b, value):
        for half in range(2):
            o_ref[h, pl.ds(2 * b + half, N, stride=4), :] = value[:, half * 128 : half * 128 + 128]

    def get(h, b):
        return jnp.concatenate([m_ref[h, pl.ds(2 * b + half, N, stride=4), :] for half in range(2)], 1)

    def change(h, b):
        hi, lo = split(p_ref[0, h * N : h * N + N, :])
        cols = slice(b * N, b * N + N)

        def dot16(u, v):
            return jnp.dot(u, v, preferred_element_type=F32)

        product = dot16(lo, chi[:, cols]) + dot16(hi, clo[:, cols]) + dot16(hi, chi[:, cols])
        put(h, b, get(h, b) - product)

    @pl.when(q > 1)
    def _():
        change(1, 0)

    @pl.when((q > 1) & (i >= q))
    def _():
        change(0, 0)

    @pl.when((q > 1) & (i < q) | (q == 1) & (i < 1))
    def _():
        put(0, 0, get(0, 0))

    @pl.when(i >= q)
    def _():
        change(1, 1)

    @pl.when(i < q)
    def _():
        put(1, 1, get(1, 1))

    put(0, 1, get(0, 1))

    for k, l_ref in enumerate((l0_ref, l1_ref)):
        cols = slice(k * N, k * N + N)

        @pl.when(q == k)
        def _(cols=cols):
            put(1, 0, p_ref[0, N:, cols])

        @pl.when((q == k) & (i > k))
        def _(cols=cols):
            put(0, 0, p_ref[0, :N, cols])

        @pl.when((q == k) & (i == k))
        def _(l_ref=l_ref):
            put(0, 0, l_ref[...])


def update(info, flat_blocks, rows, own, other, l0, w0, p10, l1, w1):
    whole = lambda *shape: pl.BlockSpec(shape, lambda t, info: (0,) * len(shape))
    tiles = pl.BlockSpec((2, 4 * N, 128), lambda t, info: (0, lax.rem(info[4] - t + 4, 4), 0))
    return pl.pallas_call(
        update_kernel,
        grid_spec=pltpu.PrefetchScalarGridSpec(
            num_scalar_prefetch=1,
            grid=(4,),
            in_specs=[tiles, pl.BlockSpec((1, 2 * N, 2 * N), lambda t, info: (t, 0, 0))]
            + [whole(2, 2 * N, N)] * 2
            + [whole(N, N)] * 5,
            out_specs=tiles,
            scratch_shapes=[pltpu.VMEM((2, 2 * N, N), F32)] + [pltpu.VMEM((2 * N, 2 * N), BF16)] * 2,
        ),
        out_shape=jax.ShapeDtypeStruct(flat_blocks.shape, F32),
        compiler_params=pltpu.CompilerParams(vmem_limit_bytes=40 << 20, dimension_semantics=("arbitrary",)),
        cost_estimate=pl.CostEstimate(flops=5 * 10**9, bytes_accessed=16 << 20, transcendentals=0),
        name="update",
    )(info, flat_blocks, rows, own, other, l0, w0, p10, l1, w1)


def after(value, *others):
    return lax.optimization_barrier((value, *others))[0]


def pick(index, options):
    out = options[0]
    for k in range(1, len(options)):
        out = jnp.where(index == k, options[k], out)
    return out


def on_device(matrix):
    row_index = lax.axis_index("row")
    col_index = lax.axis_index("col")
    y, core = row_index // NC, row_index % NC
    x, z = col_index // NZ, col_index % NZ
    flat_blocks = matrix.reshape(8 * N * 4, 128)
    column = first_column(flat_blocks)

    arrived = [
        send(column[d], lambda y, c, x, z, d=d: (y, c, (x + d) % NX, z) if z < 2 else None) for d in (1, 2, 3)
    ]

    own_rows = lax.all_to_all(column[0, 0].reshape(32, 8, N), "col", 0, 0, tiled=True)[:2]

    quarter = after(pick(x, [column[0], *arrived]), own_rows)

    parts = quarter.reshape(4, 128, N)
    sent = [
        send(
            lax.dynamic_index_in_dim(parts, (z // 2 + d) % 4, 0, keepdims=False),
            lambda y, c, x, z, d=d: (y, c, x, (z + 2 * d) % NZ) if z < 2 else None,
        )
        for d in (1, 2, 3)
    ]
    piece = pick(z // 2, [parts[0], *sent])
    tile_rows = lax.all_to_all(jnp.broadcast_to(own_rows[None], (8, 2, 8, N)), "row", 0, 0, tiled=True)
    lead, middle, last = tile_rows[0, 0], tile_rows[1, 0], tile_rows[1, 1]
    core_rows = jnp.where(
        core == 0, jnp.concatenate([lead, middle[:4]], 0), jnp.concatenate([last, middle[4:]], 0)
    )
    pieces = [piece] + [send(piece, lambda y, c, x, z, d=d: (y, c, x, (z + 2 * d) % NZ)) for d in (1, 2, 3)]
    ordered = jnp.stack([pieces[0], pieces[3], pieces[2], pieces[1]] * 2)
    mine = lax.dynamic_slice_in_dim(ordered, (4 - z // 2) % 4, 4, 0).reshape(2 * N, N)
    piece, core_rows = lax.optimization_barrier((piece, core_rows))
    core_rows = lax.all_to_all(jnp.broadcast_to(core_rows[None], (32, 12, N)), "col", 0, 0, tiled=True)
    other_rows = send(core_rows, lambda y, c, x, z: (y, 1 - c, x, z))
    mine = after(mine, other_rows)

    own_quarters = [mine] + [send(mine, lambda y, c, x, z, d=d: (y, c, (x + d) % NX, z)) for d in (1, 2, 3)]
    others = send(mine, lambda y, c, x, z: (y, c, x, z ^ 1))
    turn = (y - z // 2 + NY) % NY
    two = send(mine, lambda y, c, x, z: ((y + 2) % NY, c, x, z))
    half = jnp.where(turn >= 2, two, mine)
    others, half, core_rows, *_ = lax.optimization_barrier((others, half, core_rows, *own_quarters))

    other_quarters = [others] + [send(others, lambda y, c, x, z, d=d: (y, c, (x + d) % NX, z)) for d in (1, 2, 3)]
    one = send(half, lambda y, c, x, z: ((y + 1) % NY, c, x, z))
    l0, w0, p10, l1, w1 = factor(core.astype(jnp.int32)[None], core_rows, other_rows)
    half = after(jnp.where(turn % 2 == 1, one, half), l1, *other_quarters)
    next_half = send(half, lambda y, c, x, z: (y, c, x, z ^ 1))
    info = jnp.stack([row_index, col_index, core == z % 2, z % 2, x]).astype(jnp.int32)
    rows = solve_rows(info, w0, p10, w1, own_quarters, other_quarters)
    next_half, rows = lax.optimization_barrier((next_half, rows))
    panel = jnp.stack([jnp.where(z % 2 == 0, half, next_half), jnp.where(z % 2 == 0, next_half, half)])
    other_panel = send(panel, lambda y, c, x, z: (y, 1 - c, x, z))

    out = update(info, flat_blocks.reshape(2, 4 * N * 4, 128), rows, panel, other_panel, l0, w0, p10, l1, w1)
    return out.reshape(matrix.shape)


def solution(mesh):
    return jax.shard_map(
        on_device,
        mesh=mesh,
        in_specs=(P(None, "row", None, None, "col", None),),
        out_specs=P(None, "row", None, None, "col", None),
        check_vma=False,
    )
```

```python
import jax
import jax.numpy as jnp
from jax import lax
from jax.experimental import pallas as pl
from jax.experimental.pallas import tpu as pltpu
from jax.sharding import PartitionSpec as P

F32 = jnp.float32
BF16 = jnp.bfloat16
N = 256
SLAB = 64
NY, NC, NX, NZ = 4, 2, 4, 8


def flat(y, c, x, z):
    return ((y * NC + c) * NX + x) * NZ + z


def pairs(fn):
    found = []
    for y in range(NY):
        for c in range(NC):
            for x in range(NX):
                for z in range(NZ):
                    to = fn(y, c, x, z)
                    if to is not None:
                        found.append((flat(y, c, x, z), flat(*to)))
    return found


def send(value, fn):
    return lax.ppermute(value, ("row", "col"), pairs(fn))


def sweep_slab(slab):
    left = [g[:, :128] for g in slab]
    right = [g[:, 128:] for g in slab]
    lane = lax.broadcasted_iota(jnp.int32, (8, 128), 1)
    sub = lax.broadcasted_iota(jnp.int32, (8, 128), 0)

    def splat(v):
        return jnp.broadcast_to(v, (8, 128))

    def assemble(rows):
        out = rows[0]
        for i in range(1, 8):
            out = jnp.where(sub == i, rows[i], out)
        return out

    z_left, z_right, u_left = [], [], []
    for s in range(len(slab)):
        a0, a1 = left[s], right[s]
        o = 8 * s
        cols = [splat(a0[:, o + j : o + j + 1]) for j in range(8)]
        d = [[splat(cols[j][i : i + 1, :]) for j in range(i + 1)] for i in range(8)]
        r0 = [splat(a0[i : i + 1, :]) for i in range(8)]
        r1 = [splat(a1[i : i + 1, :]) for i in range(8)]
        in_block = (lane >= o) & (lane < o + 8)
        r = []
        l = [[None] * 8 for _ in range(8)]
        zl, zr, ul = [], [], []
        for k in range(8):
            rk = lax.rsqrt(d[k][k])
            r.append(rk)
            for i in range(k + 1, 8):
                l[i][k] = d[i][k] * rk
            for j in range(k + 1, 8):
                for i in range(j, 8):
                    d[i][j] = d[i][j] - l[i][k] * l[j][k]
            x0 = jnp.where(in_block, jnp.where(lane == o + k, 1.0, 0.0).astype(F32), r0[k])
            x1 = r1[k]
            x2 = r0[k]
            for m in range(k):
                x0 = x0 - l[k][m] * zl[m]
                x1 = x1 - l[k][m] * zr[m]
                x2 = x2 - l[k][m] * ul[m]
            zl.append(x0 * rk)
            zr.append(x1 * rk)
            ul.append(x2 * rk)
        z_left.append(assemble(zl))
        z_right.append(assemble(zr))
        u_left.append(assemble(ul))
        for t in range(s + 1, len(slab)):
            coef = []
            for k in range(8):
                c = splat(left[t][:, o + k : o + k + 1])
                for m in range(k):
                    c = c - l[k][m] * coef[m]
                coef.append(c * r[k])
            x0 = jnp.where(in_block, 0.0, left[t])
            x1 = right[t]
            for k in range(8):
                x0 = x0 - coef[k] * zl[k]
                x1 = x1 - coef[k] * zr[k]
            left[t] = x0
            right[t] = x1
    return z_left, z_right, u_left


def factor_tile(m_ref, u_ref):
    row = lax.broadcasted_iota(jnp.int32, (N, N), 0)
    lan = lax.broadcasted_iota(jnp.int32, (N, N), 1)
    row_s = lax.broadcasted_iota(jnp.int32, (SLAB, N), 0)
    lan_s = lax.broadcasted_iota(jnp.int32, (SLAB, N), 1)

    @pl.loop(0, N // SLAB)
    def _(b):
        o = b * SLAB
        rows = pl.ds(pl.multiple_of(o, SLAB), SLAB)
        slab = pltpu.roll(m_ref[rows, :], N - o, 1)
        zl, zr, ul = sweep_slab([slab[8 * g : 8 * g + 8, :] for g in range(SLAB // 8)])
        zr = jnp.concatenate(zr, 0)
        z = jnp.concatenate([jnp.concatenate(zl, 0), zr], 1)
        u = jnp.concatenate([jnp.concatenate(ul, 0), zr], 1)
        z = jnp.where((lan_s < SLAB) & (lan_s > row_s), 0.0, z)
        z = pltpu.roll(z, o, 1)
        u = pltpu.roll(u, o, 1)
        u_ref[rows, :] = u

        @pl.when(b < N // SLAB - 1)
        def _():
            coef = jnp.where(lan_s >= o + SLAB, u, 0.0)
            update = lax.dot_general(
                coef, z, (((0,), (0,)), ((), ())), precision=lax.Precision.HIGHEST, preferred_element_type=F32
            )
            m = m_ref[...]
            m = jnp.where((row >= o + SLAB) & (lan >= o) & (lan < o + SLAB), 0.0, m)
            m_ref[...] = m - update

        m_ref[rows, :] = z


def dot_nt(a, b):
    return lax.dot_general(a, b, (((1,), (1,)), ((), ())), precision=lax.Precision.HIGHEST, preferred_element_type=F32)


def read_out(l_ref, w_ref, m_ref, u_ref):
    row = lax.broadcasted_iota(jnp.int32, (N, N), 0)
    lan = lax.broadcasted_iota(jnp.int32, (N, N), 1)
    l_ref[...] = jnp.where(row >= lan, u_ref[...].T, 0.0)
    w_ref[...] = jnp.where(row >= lan, m_ref[...], 0.0)


def factor_kernel(core_ref, own_ref, other_ref, l0_out, w0_out, p10_out, l1_out, w1_out, m_ref, u_ref, tiles, sem):
    l0_ref, w0_ref, p10_ref, l1_ref, w1_ref = (tiles.at[k] for k in range(5))
    outs = (l0_out, w0_out, p10_out, l1_out, w1_out)
    copies = [pltpu.make_async_copy(tiles.at[k], out, sem.at[k]) for k, out in enumerate(outs)]
    row = lax.broadcasted_iota(jnp.int32, (N, N), 0)
    lan = lax.broadcasted_iota(jnp.int32, (N, N), 1)

    def part(core, k, lo=0, hi=8):
        return jnp.where(core_ref[0] == core, own_ref[:, k, lo:hi, :], other_ref[:, k, lo:hi, :])

    def mirrored(core):
        t = jnp.concatenate([part(core, k).reshape(N, 128) for k in range(2)], 1)
        return jnp.where(row >= lan, t, t.T)

    def between():
        sides = [jnp.concatenate([part(core, 2, lo, lo + 4) for core in range(2)], 1) for lo in (0, 4)]
        return jnp.concatenate([side.reshape(N, 128) for side in sides], 1)

    m_ref[...] = mirrored(0)
    factor_tile(m_ref, u_ref)
    read_out(l0_ref, w0_ref, m_ref, u_ref)
    p10 = dot_nt(between(), w0_ref[...])
    p10_ref[...] = p10
    for copy in copies[:3]:
        copy.start()
    m_ref[...] = mirrored(1) - dot_nt(p10, p10)
    factor_tile(m_ref, u_ref)
    read_out(l1_ref, w1_ref, m_ref, u_ref)
    for copy in copies[3:]:
        copy.start()
    for copy in copies:
        copy.wait()


def factor(core, own, other):
    vmem = pl.BlockSpec(memory_space=pltpu.VMEM)
    return pl.pallas_call(
        factor_kernel,
        out_shape=[jax.ShapeDtypeStruct((N, N), F32)] * 5,
        in_specs=[pl.BlockSpec(memory_space=pltpu.SMEM), vmem, vmem],
        out_specs=[pl.BlockSpec(memory_space=pltpu.HBM)] * 5,
        scratch_shapes=[pltpu.VMEM((N, N), F32)] * 2 + [pltpu.VMEM((5, N, N), F32), pltpu.SemaphoreType.DMA((5,))],
        compiler_params=pltpu.CompilerParams(vmem_limit_bytes=60 << 20),
        cost_estimate=pl.CostEstimate(flops=10**9, bytes_accessed=60 << 20, transcendentals=0),
        name="factor",
    )(core, own, other)


def column_kernel(m_ref, o_ref):
    for half in range(2):
        o_ref[0, 0, :, half * 128 : half * 128 + 128] = m_ref[pl.ds(half, N, stride=4), :]


def first_column(flat_blocks):
    return pl.pallas_call(
        column_kernel,
        grid=(8,),
        out_shape=jax.ShapeDtypeStruct((4, 2, N, N), F32),
        in_specs=[pl.BlockSpec((4 * N, 128), lambda a: (a, 0))],
        out_specs=pl.BlockSpec((1, 1, N, N), lambda a: (a % 4, a // 4, 0, 0)),
        compiler_params=pltpu.CompilerParams(vmem_limit_bytes=16 << 20, dimension_semantics=("arbitrary",)),
        cost_estimate=pl.CostEstimate(flops=0, bytes_accessed=6 << 20, transcendentals=0),
        name="first_column",
    )(flat_blocks)


def order_kernel(slot_ref, *refs):
    pieces, o_ref = refs[:-1], refs[-1]
    for d, piece in enumerate(pieces):
        slot = lax.rem(slot_ref[0] + len(pieces) - d, len(pieces))
        o_ref[pl.ds(pl.multiple_of(slot * 128, 128), 128), :] = piece[...]


def order(slot, pieces):
    return pl.pallas_call(
        order_kernel,
        out_shape=jax.ShapeDtypeStruct((2 * N, N), F32),
        in_specs=[pl.BlockSpec(memory_space=pltpu.SMEM)] + [pl.BlockSpec(memory_space=pltpu.VMEM)] * 4,
        out_specs=pl.BlockSpec(memory_space=pltpu.VMEM),
        compiler_params=pltpu.CompilerParams(vmem_limit_bytes=8 << 20),
        cost_estimate=pl.CostEstimate(flops=0, bytes_accessed=1 << 20, transcendentals=0),
        name="order",
    )(slot, *pieces)


def split(v):
    hi = v.astype(BF16)
    return hi, (v - hi.astype(F32)).astype(BF16)


def split3(v):
    hi = v.astype(BF16)
    rest = v - hi.astype(F32)
    mid = rest.astype(BF16)
    return hi, mid, (rest - mid.astype(F32)).astype(BF16)


def six_left(v):
    hi, mid, lo = split3(v)
    return jnp.concatenate([lo, hi, mid, mid, hi, hi], 1)


def six_right(v):
    hi, mid, lo = split3(v)
    return jnp.concatenate([hi, lo, mid, hi, mid, hi], 0)


def dot16(a, b):
    return jnp.dot(a, b, preferred_element_type=F32)


def dot_nn(a, b):
    return jnp.dot(a, b, precision=lax.Precision.HIGHEST, preferred_element_type=F32)


def own_kernel(info_ref, w0_ref, p10_ref, w1_ref, a0, a1, a2, a3, o_ref, turned_ref, w_s):
    t = pl.program_id(0)

    @pl.when(t == 0)
    def _():
        turned_ref[...] = dot_nn(w1_ref[...], p10_ref[...])
        w_s[...] = six_right(jnp.where(info_ref[3] == 0, w0_ref[...], w1_ref[...]).T)

    for d, mine in enumerate((a0, a1, a2, a3)):
        @pl.when(t == d)
        def _(mine=mine):
            o_ref[0] = dot16(six_left(mine[...]), w_s[...])


def solve_own(info, w0, p10, w1, own_quarters):
    whole = lambda *shape: pl.BlockSpec(shape, lambda t: (0,) * len(shape))
    return pl.pallas_call(
        own_kernel,
        grid=(4,),
        in_specs=[pl.BlockSpec(memory_space=pltpu.SMEM)] + [whole(N, N)] * 3 + [whole(2 * N, N)] * 4,
        out_specs=[pl.BlockSpec((1, 2 * N, N), lambda t: (t, 0, 0)), whole(N, N)],
        out_shape=[jax.ShapeDtypeStruct((4, 2 * N, N), F32), jax.ShapeDtypeStruct((N, N), F32)],
        scratch_shapes=[pltpu.VMEM((6 * N, N), BF16)],
        compiler_params=pltpu.CompilerParams(vmem_limit_bytes=60 << 20, dimension_semantics=("arbitrary",)),
        cost_estimate=pl.CostEstimate(flops=2 * 10**9, bytes_accessed=60 << 20, transcendentals=0),
        name="solve_own",
    )(info, w0, p10, w1, *own_quarters)


def rows_kernel(info_ref, w0_ref, w1_ref, turned_ref, part_ref, others_ref, lower_ref, u1, u2, u3, o_ref, w_s, t_s):
    t = pl.program_id(0)
    even = info_ref[3] == 0

    @pl.when(t == 0)
    def _():
        w_s[...] = six_right(jnp.where(even, w1_ref[...], w0_ref[...]).T)
        t_s[...] = six_right(turned_ref[...].T)

    for d, upper in enumerate((None, u1, u2, u3)):
        @pl.when(t == d)
        def _(d=d, upper=upper):
            if d == 0:
                others = others_ref[...]
            else:
                others = jnp.concatenate([lower_ref[d * N - N : d * N, :], upper[...]], 0)
            part = part_ref[0]
            rest = dot16(six_left(others), w_s[...])
            first = jnp.where(even, part, rest)
            o_ref[0, :, :N] = first
            o_ref[0, :, N:] = jnp.where(even, rest, part) - dot16(six_left(first), t_s[...])


def solve_rows(info, w0, w1, turned, part, others, lower, upper):
    whole = lambda *shape: pl.BlockSpec(shape, lambda t: (0,) * len(shape))
    return pl.pallas_call(
        rows_kernel,
        grid=(4,),
        in_specs=[pl.BlockSpec(memory_space=pltpu.SMEM)]
        + [whole(N, N)] * 3
        + [pl.BlockSpec((1, 2 * N, N), lambda t: (t, 0, 0)), whole(2 * N, N), whole(3 * N, N)]
        + [whole(N, N)] * 3,
        out_specs=pl.BlockSpec((1, 2 * N, 2 * N), lambda t: (t, 0, 0)),
        out_shape=jax.ShapeDtypeStruct((4, 2 * N, 2 * N), F32),
        scratch_shapes=[pltpu.VMEM((6 * N, N), BF16)] * 2,
        compiler_params=pltpu.CompilerParams(vmem_limit_bytes=60 << 20, dimension_semantics=("arbitrary",)),
        cost_estimate=pl.CostEstimate(flops=5 * 10**9, bytes_accessed=9 << 20, transcendentals=0),
        name="solve_rows",
    )(info, w0, w1, turned, part, others, lower, *upper)


def update_kernel(
    info_ref, m_ref, p_ref, own_ref, other_ref, l0_ref, w0_ref, p10_ref, l1_ref, w1_ref, o_ref, x_s, chi, clo
):
    t = pl.program_id(0)
    p, q, keep_own, x = info_ref[0], info_ref[1], info_ref[2], info_ref[4]
    i = 8 * lax.rem(x - t + 4, 4) + p

    @pl.when(t == 0)
    def _():
        for value, kept in ((own_ref, 1), (other_ref, 0)):
            @pl.when(keep_own == kept)
            def _(value=value):
                x_s[...] = value[...]

        first = dot_nt(w0_ref[...], x_s[0])
        second = dot_nn(w1_ref[...], x_s[1].T - dot_nn(p10_ref[...], first))
        for k, panel in enumerate((first, second)):
            hi, lo = split(panel)
            chi[k * N : k * N + N, :] = hi
            clo[k * N : k * N + N, :] = lo

    def put(h, b, value):
        for half in range(2):
            o_ref[h, pl.ds(2 * b + half, N, stride=4), :] = value[:, half * 128 : half * 128 + 128]

    def get(h, b):
        return jnp.concatenate([m_ref[h, pl.ds(2 * b + half, N, stride=4), :] for half in range(2)], 1)

    def change(h, b):
        hi, lo = split(p_ref[0, h * N : h * N + N, :])
        cols = slice(b * N, b * N + N)

        product = dot16(lo, chi[:, cols]) + dot16(hi, clo[:, cols]) + dot16(hi, chi[:, cols])
        put(h, b, get(h, b) - product)

    @pl.when(q > 1)
    def _():
        change(1, 0)

    @pl.when((q > 1) & (i >= q))
    def _():
        change(0, 0)

    @pl.when((q > 1) & (i < q) | (q == 1) & (i < 1))
    def _():
        put(0, 0, get(0, 0))

    @pl.when(i >= q)
    def _():
        change(1, 1)

    @pl.when(i < q)
    def _():
        put(1, 1, get(1, 1))

    put(0, 1, get(0, 1))

    for k, l_ref in enumerate((l0_ref, l1_ref)):
        cols = slice(k * N, k * N + N)

        @pl.when(q == k)
        def _(cols=cols):
            put(1, 0, p_ref[0, N:, cols])

        @pl.when((q == k) & (i > k))
        def _(cols=cols):
            put(0, 0, p_ref[0, :N, cols])

        @pl.when((q == k) & (i == k))
        def _(l_ref=l_ref):
            put(0, 0, l_ref[...])


def update(info, flat_blocks, rows, own, other, l0, w0, p10, l1, w1):
    whole = lambda *shape: pl.BlockSpec(shape, lambda t, info: (0,) * len(shape))
    tiles = pl.BlockSpec((2, 4 * N, 128), lambda t, info: (0, lax.rem(info[4] - t + 4, 4), 0))
    return pl.pallas_call(
        update_kernel,
        grid_spec=pltpu.PrefetchScalarGridSpec(
            num_scalar_prefetch=1,
            grid=(4,),
            in_specs=[tiles, pl.BlockSpec((1, 2 * N, 2 * N), lambda t, info: (t, 0, 0))]
            + [whole(2, 2 * N, N)] * 2
            + [whole(N, N)] * 5,
            out_specs=tiles,
            scratch_shapes=[pltpu.VMEM((2, 2 * N, N), F32)] + [pltpu.VMEM((2 * N, 2 * N), BF16)] * 2,
        ),
        out_shape=jax.ShapeDtypeStruct(flat_blocks.shape, F32),
        compiler_params=pltpu.CompilerParams(vmem_limit_bytes=40 << 20, dimension_semantics=("arbitrary",)),
        cost_estimate=pl.CostEstimate(flops=5 * 10**9, bytes_accessed=16 << 20, transcendentals=0),
        name="update",
    )(info, flat_blocks, rows, own, other, l0, w0, p10, l1, w1)


def after(value, *others):
    return lax.optimization_barrier((value, *others))[0]


def pick(index, options):
    out = options[0]
    for k in range(1, len(options)):
        out = jnp.where(index == k, options[k], out)
    return out


def on_device(matrix):
    row_index = lax.axis_index("row")
    col_index = lax.axis_index("col")
    y, core = row_index // NC, row_index % NC
    x, z = col_index // NZ, col_index % NZ
    flat_blocks = matrix.reshape(8 * N * 4, 128)
    column = first_column(flat_blocks)

    arrived = [
        send(column[d], lambda y, c, x, z, d=d: (y, c, d, z) if x == 0 and z < 2 else None) for d in (1, 2, 3)
    ]

    own_rows = lax.all_to_all(column[0, 0].reshape(32, 8, N), "col", 0, 0, tiled=True)[:2]

    quarter = after(pick(x, [column[0], *arrived]), own_rows)

    parts = quarter.reshape(4, 128, N)
    sent = [
        send(
            lax.dynamic_index_in_dim(parts, (z // 2 + d) % 4, 0, keepdims=False),
            lambda y, c, x, z, d=d: (y, c, x, (z + 2 * d) % NZ) if z < 2 else None,
        )
        for d in (1, 2, 3)
    ]
    piece = pick(z // 2, [parts[0], *sent])
    tile_rows = lax.all_to_all(jnp.broadcast_to(own_rows[None], (8, 2, 8, N)), "row", 0, 0, tiled=True)
    lead, middle, last = tile_rows[0, 0], tile_rows[1, 0], tile_rows[1, 1]
    whole, part = jnp.where(core == 0, lead, last), jnp.where(core == 0, middle[:4], middle[4:])
    core_rows = jnp.stack([whole[:, :128], whole[:, 128:], jnp.concatenate([part[:, :128], part[:, 128:]], 0)])
    piece, core_rows = lax.optimization_barrier((piece, core_rows))
    pieces = [piece] + [send(piece, lambda y, c, x, z, d=d: (y, c, x, (z + 2 * d) % NZ)) for d in (1, 2, 3)]
    mine = order((z // 2).astype(jnp.int32)[None], pieces)
    core_rows = lax.all_to_all(jnp.broadcast_to(core_rows[None], (32, 3, 8, 128)), "col", 0, 0, tiled=True)
    mine, core_rows = lax.optimization_barrier((mine, core_rows))
    other_rows = send(core_rows, lambda y, c, x, z: (y, 1 - c, x, z))

    own_quarters = [mine] + [send(mine, lambda y, c, x, z, d=d: (y, c, (x + d) % NX, z)) for d in (1, 2, 3)]
    others = send(mine, lambda y, c, x, z: (y, c, x, z ^ 1))
    turn = (y - z // 2 + NY) % NY
    two = send(mine, lambda y, c, x, z: ((y + 2) % NY, c, x, z))
    half = jnp.where(turn >= 2, two, mine)
    l0, w0, p10, l1, w1 = factor(core.astype(jnp.int32)[None], core_rows, other_rows)
    others, half, *_ = lax.optimization_barrier((others, half, l1, *own_quarters))

    upper = [send(others[N:], lambda y, c, x, z, d=d: (y, c, (x + d) % NX, z)) for d in (1, 2, 3)]
    lower = send(jnp.concatenate([q[:N] for q in own_quarters[1:]], 0), lambda y, c, x, z: (y, c, x, z ^ 1))
    one = send(half, lambda y, c, x, z: ((y + 1) % NY, c, x, z))
    info = jnp.stack([row_index, col_index, core == z % 2, z % 2, x]).astype(jnp.int32)
    first_part, turned = solve_own(info, w0, p10, w1, own_quarters)
    one, half, *_ = lax.optimization_barrier((one, half, first_part, lower, *upper))
    half = jnp.where(turn % 2 == 1, one, half)
    next_half = send(half, lambda y, c, x, z: (y, c, x, z ^ 1))
    rows = solve_rows(info, w0, w1, turned, first_part, others, lower, upper)
    next_half, rows = lax.optimization_barrier((next_half, rows))
    panel = jnp.stack([jnp.where(z % 2 == 0, half, next_half), jnp.where(z % 2 == 0, next_half, half)])
    other_panel = send(panel, lambda y, c, x, z: (y, 1 - c, x, z))

    out = update(info, flat_blocks.reshape(2, 4 * N * 4, 128), rows, panel, other_panel, l0, w0, p10, l1, w1)
    return out.reshape(matrix.shape)


def solution(mesh):
    return jax.shard_map(
        on_device,
        mesh=mesh,
        in_specs=(P(None, "row", None, None, "col", None),),
        out_specs=P(None, "row", None, None, "col", None),
        check_vma=False,
    )
```

```python
import jax
import jax.numpy as jnp
from jax import lax
from jax.experimental import pallas as pl
from jax.experimental.pallas import tpu as pltpu
from jax.sharding import PartitionSpec as P

F32 = jnp.float32
BF16 = jnp.bfloat16
N = 256
SLAB = 64
NY, NC, NX, NZ = 4, 2, 4, 8


def flat(y, c, x, z):
    return ((y * NC + c) * NX + x) * NZ + z


def pairs(fn):
    found = []
    for y in range(NY):
        for c in range(NC):
            for x in range(NX):
                for z in range(NZ):
                    to = fn(y, c, x, z)
                    if to is not None:
                        found.append((flat(y, c, x, z), flat(*to)))
    return found


def send(value, fn):
    return lax.ppermute(value, ("row", "col"), pairs(fn))


def sweep_slab(slab):
    left = [g[:, :128] for g in slab]
    right = [g[:, 128:] for g in slab]
    lane = lax.broadcasted_iota(jnp.int32, (8, 128), 1)
    sub = lax.broadcasted_iota(jnp.int32, (8, 128), 0)

    def splat(v):
        return jnp.broadcast_to(v, (8, 128))

    def assemble(rows):
        out = rows[0]
        for i in range(1, 8):
            out = jnp.where(sub == i, rows[i], out)
        return out

    z_left, z_right, u_left = [], [], []
    for s in range(len(slab)):
        a0, a1 = left[s], right[s]
        o = 8 * s
        cols = [splat(a0[:, o + j : o + j + 1]) for j in range(8)]
        d = [[splat(cols[j][i : i + 1, :]) for j in range(i + 1)] for i in range(8)]
        r0 = [splat(a0[i : i + 1, :]) for i in range(8)]
        r1 = [splat(a1[i : i + 1, :]) for i in range(8)]
        in_block = (lane >= o) & (lane < o + 8)
        r = []
        l = [[None] * 8 for _ in range(8)]
        zl, zr, ul = [], [], []
        for k in range(8):
            rk = lax.rsqrt(d[k][k])
            r.append(rk)
            for i in range(k + 1, 8):
                l[i][k] = d[i][k] * rk
            for j in range(k + 1, 8):
                for i in range(j, 8):
                    d[i][j] = d[i][j] - l[i][k] * l[j][k]
            x0 = jnp.where(in_block, jnp.where(lane == o + k, 1.0, 0.0).astype(F32), r0[k])
            x1 = r1[k]
            x2 = r0[k]
            for m in range(k):
                x0 = x0 - l[k][m] * zl[m]
                x1 = x1 - l[k][m] * zr[m]
                x2 = x2 - l[k][m] * ul[m]
            zl.append(x0 * rk)
            zr.append(x1 * rk)
            ul.append(x2 * rk)
        z_left.append(assemble(zl))
        z_right.append(assemble(zr))
        u_left.append(assemble(ul))
        for t in range(s + 1, len(slab)):
            coef = []
            for k in range(8):
                c = splat(left[t][:, o + k : o + k + 1])
                for m in range(k):
                    c = c - l[k][m] * coef[m]
                coef.append(c * r[k])
            x0 = jnp.where(in_block, 0.0, left[t])
            x1 = right[t]
            for k in range(8):
                x0 = x0 - coef[k] * zl[k]
                x1 = x1 - coef[k] * zr[k]
            left[t] = x0
            right[t] = x1
    return z_left, z_right, u_left


def factor_tile(m_ref, u_ref):
    row = lax.broadcasted_iota(jnp.int32, (N, N), 0)
    lan = lax.broadcasted_iota(jnp.int32, (N, N), 1)
    row_s = lax.broadcasted_iota(jnp.int32, (SLAB, N), 0)
    lan_s = lax.broadcasted_iota(jnp.int32, (SLAB, N), 1)

    @pl.loop(0, N // SLAB)
    def _(b):
        o = b * SLAB
        rows = pl.ds(pl.multiple_of(o, SLAB), SLAB)
        slab = pltpu.roll(m_ref[rows, :], N - o, 1)
        zl, zr, ul = sweep_slab([slab[8 * g : 8 * g + 8, :] for g in range(SLAB // 8)])
        zr = jnp.concatenate(zr, 0)
        z = jnp.concatenate([jnp.concatenate(zl, 0), zr], 1)
        u = jnp.concatenate([jnp.concatenate(ul, 0), zr], 1)
        z = jnp.where((lan_s < SLAB) & (lan_s > row_s), 0.0, z)
        z = pltpu.roll(z, o, 1)
        u = pltpu.roll(u, o, 1)
        u_ref[rows, :] = u

        @pl.when(b < N // SLAB - 1)
        def _():
            coef = jnp.where(lan_s >= o + SLAB, u, 0.0)
            update = lax.dot_general(
                coef, z, (((0,), (0,)), ((), ())), precision=lax.Precision.HIGHEST, preferred_element_type=F32
            )
            m = m_ref[...]
            m = jnp.where((row >= o + SLAB) & (lan >= o) & (lan < o + SLAB), 0.0, m)
            m_ref[...] = m - update

        m_ref[rows, :] = z


def dot_nt(a, b):
    return lax.dot_general(a, b, (((1,), (1,)), ((), ())), precision=lax.Precision.HIGHEST, preferred_element_type=F32)


def read_out(l_ref, w_ref, m_ref, u_ref):
    row = lax.broadcasted_iota(jnp.int32, (N, N), 0)
    lan = lax.broadcasted_iota(jnp.int32, (N, N), 1)
    l_ref[...] = jnp.where(row >= lan, u_ref[...].T, 0.0)
    w_ref[...] = jnp.where(row >= lan, m_ref[...], 0.0)


def factor_kernel(core_ref, own_ref, other_ref, l0_out, w0_out, p10_out, l1_out, w1_out, m_ref, u_ref, tiles, sem):
    l0_ref, w0_ref, p10_ref, l1_ref, w1_ref = (tiles.at[k] for k in range(5))
    outs = (l0_out, w0_out, p10_out, l1_out, w1_out)
    copies = [pltpu.make_async_copy(tiles.at[k], out, sem.at[k]) for k, out in enumerate(outs)]
    row = lax.broadcasted_iota(jnp.int32, (N, N), 0)
    lan = lax.broadcasted_iota(jnp.int32, (N, N), 1)

    def part(core, k, lo=0, hi=8):
        return jnp.where(core_ref[0] == core, own_ref[:, k, lo:hi, :], other_ref[:, k, lo:hi, :])

    def mirrored(core):
        t = jnp.concatenate([part(core, k).reshape(N, 128) for k in range(2)], 1)
        return jnp.where(row >= lan, t, t.T)

    def between():
        sides = [jnp.concatenate([part(core, 2, lo, lo + 4) for core in range(2)], 1) for lo in (0, 4)]
        return jnp.concatenate([side.reshape(N, 128) for side in sides], 1)

    m_ref[...] = mirrored(0)
    factor_tile(m_ref, u_ref)
    read_out(l0_ref, w0_ref, m_ref, u_ref)
    p10 = dot_nt(between(), w0_ref[...])
    p10_ref[...] = p10
    for copy in copies[:3]:
        copy.start()
    m_ref[...] = mirrored(1) - dot_nt(p10, p10)
    factor_tile(m_ref, u_ref)
    read_out(l1_ref, w1_ref, m_ref, u_ref)
    for copy in copies[3:]:
        copy.start()
    for copy in copies:
        copy.wait()


def factor(core, own, other):
    vmem = pl.BlockSpec(memory_space=pltpu.VMEM)
    return pl.pallas_call(
        factor_kernel,
        out_shape=[jax.ShapeDtypeStruct((N, N), F32)] * 5,
        in_specs=[pl.BlockSpec(memory_space=pltpu.SMEM), vmem, vmem],
        out_specs=[pl.BlockSpec(memory_space=pltpu.HBM)] * 5,
        scratch_shapes=[pltpu.VMEM((N, N), F32)] * 2 + [pltpu.VMEM((5, N, N), F32), pltpu.SemaphoreType.DMA((5,))],
        compiler_params=pltpu.CompilerParams(vmem_limit_bytes=60 << 20),
        cost_estimate=pl.CostEstimate(flops=10**9, bytes_accessed=60 << 20, transcendentals=0),
        name="factor",
    )(core, own, other)


def column_kernel(m_ref, *o_refs):
    for d, o_ref in enumerate(o_refs):
        @pl.when(pl.program_id(0) == d)
        def _(o_ref=o_ref):
            for half in range(2):
                o_ref[0, :, half * 128 : half * 128 + 128] = m_ref[pl.ds(half, N, stride=4), :]


def first_column(flat_blocks):
    out = lambda d: pl.BlockSpec((1, N, N), lambda k, h: (jnp.where(k == d, h, jnp.where(k < d, 0, 1)), 0, 0))
    return pl.pallas_call(
        column_kernel,
        grid=(4, 2),
        out_shape=[jax.ShapeDtypeStruct((2, N, N), F32)] * 4,
        in_specs=[pl.BlockSpec((4 * N, 128), lambda k, h: (k + 4 * h, 0))],
        out_specs=[out(d) for d in range(4)],
        compiler_params=pltpu.CompilerParams(
            vmem_limit_bytes=16 << 20, dimension_semantics=("arbitrary", "arbitrary")
        ),
        cost_estimate=pl.CostEstimate(flops=0, bytes_accessed=6 << 20, transcendentals=0),
        name="first_column",
    )(flat_blocks)


def order_kernel(slot_ref, *refs):
    pieces, o_ref = refs[:-1], refs[-1]
    for d, piece in enumerate(pieces):
        slot = lax.rem(slot_ref[0] + len(pieces) - d, len(pieces))
        o_ref[pl.ds(pl.multiple_of(slot * 128, 128), 128), :] = piece[...]


def order(slot, pieces):
    return pl.pallas_call(
        order_kernel,
        out_shape=jax.ShapeDtypeStruct((2 * N, N), F32),
        in_specs=[pl.BlockSpec(memory_space=pltpu.SMEM)] + [pl.BlockSpec(memory_space=pltpu.VMEM)] * 4,
        out_specs=pl.BlockSpec(memory_space=pltpu.VMEM),
        compiler_params=pltpu.CompilerParams(vmem_limit_bytes=8 << 20),
        cost_estimate=pl.CostEstimate(flops=0, bytes_accessed=1 << 20, transcendentals=0),
        name="order",
    )(slot, *pieces)


def split(v):
    hi = v.astype(BF16)
    return hi, (v - hi.astype(F32)).astype(BF16)


def split3(v):
    hi = v.astype(BF16)
    rest = v - hi.astype(F32)
    mid = rest.astype(BF16)
    return hi, mid, (rest - mid.astype(F32)).astype(BF16)


def six_left(v):
    hi, mid, lo = split3(v)
    return jnp.concatenate([lo, hi, mid, mid, hi, hi], 1)


def six_right(v):
    hi, mid, lo = split3(v)
    return jnp.concatenate([hi, lo, mid, hi, mid, hi], 0)


def dot16(a, b):
    return jnp.dot(a, b, preferred_element_type=F32)


def dot_nn(a, b):
    return jnp.dot(a, b, precision=lax.Precision.HIGHEST, preferred_element_type=F32)


def own_kernel(info_ref, w0_ref, p10_ref, w1_ref, a0, a1, a2, a3, o_ref, turned_ref, w_s):
    t = pl.program_id(0)

    @pl.when(t == 0)
    def _():
        turned_ref[...] = dot_nn(w1_ref[...], p10_ref[...])
        w_s[...] = six_right(jnp.where(info_ref[3] == 0, w0_ref[...], w1_ref[...]).T)

    for d, mine in enumerate((a0, a1, a2, a3)):
        @pl.when(t == d)
        def _(mine=mine):
            o_ref[0] = dot16(six_left(mine[...]), w_s[...])


def solve_own(info, w0, p10, w1, own_quarters):
    whole = lambda *shape: pl.BlockSpec(shape, lambda t: (0,) * len(shape))
    return pl.pallas_call(
        own_kernel,
        grid=(4,),
        in_specs=[pl.BlockSpec(memory_space=pltpu.SMEM)] + [whole(N, N)] * 3 + [whole(2 * N, N)] * 4,
        out_specs=[pl.BlockSpec((1, 2 * N, N), lambda t: (t, 0, 0)), whole(N, N)],
        out_shape=[jax.ShapeDtypeStruct((4, 2 * N, N), F32), jax.ShapeDtypeStruct((N, N), F32)],
        scratch_shapes=[pltpu.VMEM((6 * N, N), BF16)],
        compiler_params=pltpu.CompilerParams(vmem_limit_bytes=60 << 20, dimension_semantics=("arbitrary",)),
        cost_estimate=pl.CostEstimate(flops=2 * 10**9, bytes_accessed=60 << 20, transcendentals=0),
        name="solve_own",
    )(info, w0, p10, w1, *own_quarters)


def rows_kernel(info_ref, w0_ref, w1_ref, turned_ref, part_ref, others_ref, lower_ref, u1, u2, u3, o_ref, w_s, t_s):
    t = pl.program_id(0)
    even = info_ref[3] == 0

    @pl.when(t == 0)
    def _():
        w_s[...] = six_right(jnp.where(even, w1_ref[...], w0_ref[...]).T)
        t_s[...] = six_right(turned_ref[...].T)

    for d, upper in enumerate((None, u1, u2, u3)):
        @pl.when(t == d)
        def _(d=d, upper=upper):
            if d == 0:
                others = others_ref[...]
            else:
                others = jnp.concatenate([lower_ref[d * N - N : d * N, :], upper[...]], 0)
            part = part_ref[0]
            rest = dot16(six_left(others), w_s[...])
            first = jnp.where(even, part, rest)
            o_ref[0, :, :N] = first
            o_ref[0, :, N:] = jnp.where(even, rest, part) - dot16(six_left(first), t_s[...])


def solve_rows(info, w0, w1, turned, part, others, lower, upper):
    whole = lambda *shape: pl.BlockSpec(shape, lambda t: (0,) * len(shape))
    return pl.pallas_call(
        rows_kernel,
        grid=(4,),
        in_specs=[pl.BlockSpec(memory_space=pltpu.SMEM)]
        + [whole(N, N)] * 3
        + [pl.BlockSpec((1, 2 * N, N), lambda t: (t, 0, 0)), whole(2 * N, N), whole(3 * N, N)]
        + [whole(N, N)] * 3,
        out_specs=pl.BlockSpec((1, 2 * N, 2 * N), lambda t: (t, 0, 0)),
        out_shape=jax.ShapeDtypeStruct((4, 2 * N, 2 * N), F32),
        scratch_shapes=[pltpu.VMEM((6 * N, N), BF16)] * 2,
        compiler_params=pltpu.CompilerParams(vmem_limit_bytes=60 << 20, dimension_semantics=("arbitrary",)),
        cost_estimate=pl.CostEstimate(flops=5 * 10**9, bytes_accessed=9 << 20, transcendentals=0),
        name="solve_rows",
    )(info, w0, w1, turned, part, others, lower, *upper)


def update_kernel(
    info_ref, m_ref, p_ref, own_ref, other_ref, l0_ref, w0_ref, p10_ref, l1_ref, w1_ref, o_ref, x_s, chi, clo
):
    t = pl.program_id(0)
    p, q, keep_own, x = info_ref[0], info_ref[1], info_ref[2], info_ref[4]
    i = 8 * lax.rem(x - t + 4, 4) + p

    @pl.when(t == 0)
    def _():
        for value, kept in ((own_ref, 1), (other_ref, 0)):
            @pl.when(keep_own == kept)
            def _(value=value):
                x_s[...] = value[...]

        first = dot_nt(w0_ref[...], x_s[0])
        second = dot_nn(w1_ref[...], x_s[1].T - dot_nn(p10_ref[...], first))
        for k, panel in enumerate((first, second)):
            hi, lo = split(panel)
            chi[k * N : k * N + N, :] = hi
            clo[k * N : k * N + N, :] = lo

    def put(h, b, value):
        for half in range(2):
            o_ref[h, pl.ds(2 * b + half, N, stride=4), :] = value[:, half * 128 : half * 128 + 128]

    def get(h, b):
        return jnp.concatenate([m_ref[h, pl.ds(2 * b + half, N, stride=4), :] for half in range(2)], 1)

    def change(h, b):
        hi, lo = split(p_ref[0, h * N : h * N + N, :])
        cols = slice(b * N, b * N + N)

        product = dot16(lo, chi[:, cols]) + dot16(hi, clo[:, cols]) + dot16(hi, chi[:, cols])
        put(h, b, get(h, b) - product)

    @pl.when(q > 1)
    def _():
        change(1, 0)

    @pl.when((q > 1) & (i >= q))
    def _():
        change(0, 0)

    @pl.when((q > 1) & (i < q) | (q == 1) & (i < 1))
    def _():
        put(0, 0, get(0, 0))

    @pl.when(i >= q)
    def _():
        change(1, 1)

    @pl.when(i < q)
    def _():
        put(1, 1, get(1, 1))

    put(0, 1, get(0, 1))

    for k, l_ref in enumerate((l0_ref, l1_ref)):
        cols = slice(k * N, k * N + N)

        @pl.when(q == k)
        def _(cols=cols):
            put(1, 0, p_ref[0, N:, cols])

        @pl.when((q == k) & (i > k))
        def _(cols=cols):
            put(0, 0, p_ref[0, :N, cols])

        @pl.when((q == k) & (i == k))
        def _(l_ref=l_ref):
            put(0, 0, l_ref[...])


def update(info, flat_blocks, rows, own, other, l0, w0, p10, l1, w1):
    whole = lambda *shape: pl.BlockSpec(shape, lambda t, info: (0,) * len(shape))
    tiles = pl.BlockSpec((2, 4 * N, 128), lambda t, info: (0, lax.rem(info[4] - t + 4, 4), 0))
    return pl.pallas_call(
        update_kernel,
        grid_spec=pltpu.PrefetchScalarGridSpec(
            num_scalar_prefetch=1,
            grid=(4,),
            in_specs=[tiles, pl.BlockSpec((1, 2 * N, 2 * N), lambda t, info: (t, 0, 0))]
            + [whole(2, 2 * N, N)] * 2
            + [whole(N, N)] * 5,
            out_specs=tiles,
            scratch_shapes=[pltpu.VMEM((2, 2 * N, N), F32)] + [pltpu.VMEM((2 * N, 2 * N), BF16)] * 2,
        ),
        out_shape=jax.ShapeDtypeStruct(flat_blocks.shape, F32),
        compiler_params=pltpu.CompilerParams(vmem_limit_bytes=40 << 20, dimension_semantics=("arbitrary",)),
        cost_estimate=pl.CostEstimate(flops=5 * 10**9, bytes_accessed=16 << 20, transcendentals=0),
        name="update",
    )(info, flat_blocks, rows, own, other, l0, w0, p10, l1, w1)


def after(value, *others):
    return lax.optimization_barrier((value, *others))[0]


def pick(index, options):
    out = options[0]
    for k in range(1, len(options)):
        out = jnp.where(index == k, options[k], out)
    return out


def on_device(matrix):
    row_index = lax.axis_index("row")
    col_index = lax.axis_index("col")
    y, core = row_index // NC, row_index % NC
    x, z = col_index // NZ, col_index % NZ
    flat_blocks = matrix.reshape(8 * N * 4, 128)
    column = first_column(flat_blocks)

    arrived = [
        send(column[d], lambda y, c, x, z, d=d: (y, c, d, z) if x == 0 and z < 2 else None) for d in (1, 2, 3)
    ]

    own_rows = lax.all_to_all(column[0][0].reshape(32, 8, N), "col", 0, 0, tiled=True)[:2]

    quarter = after(pick(x, [column[0], *arrived]), own_rows)

    parts = quarter.reshape(4, 128, N)
    sent = [
        send(
            lax.dynamic_index_in_dim(parts, (z // 2 + d) % 4, 0, keepdims=False),
            lambda y, c, x, z, d=d: (y, c, x, (z + 2 * d) % NZ) if z < 2 else None,
        )
        for d in (1, 2, 3)
    ]
    piece = pick(z // 2, [parts[0], *sent])
    tile_rows = after(own_rows, quarter)
    tile_rows = lax.all_to_all(jnp.broadcast_to(tile_rows[None], (8, 2, 8, N)), "row", 0, 0, tiled=True)
    lead, middle, last = tile_rows[0, 0], tile_rows[1, 0], tile_rows[1, 1]
    whole, part = jnp.where(core == 0, lead, last), jnp.where(core == 0, middle[:4], middle[4:])
    core_rows = jnp.stack([whole[:, :128], whole[:, 128:], jnp.concatenate([part[:, :128], part[:, 128:]], 0)])
    core_rows = lax.all_to_all(jnp.broadcast_to(core_rows[None], (32, 3, 8, 128)), "col", 0, 0, tiled=True)
    piece, core_rows = lax.optimization_barrier((piece, core_rows))
    pieces = [piece] + [send(piece, lambda y, c, x, z, d=d: (y, c, x, (z + 2 * d) % NZ)) for d in (1, 2, 3)]
    mine = order((z // 2).astype(jnp.int32)[None], pieces)
    other_rows = send(core_rows, lambda y, c, x, z: (y, 1 - c, x, z))
    mine, other_rows = lax.optimization_barrier((mine, other_rows))

    own_quarters = [mine] + [send(mine, lambda y, c, x, z, d=d: (y, c, (x + d) % NX, z)) for d in (1, 2, 3)]
    others = send(mine, lambda y, c, x, z: (y, c, x, z ^ 1))
    turn = (y - z // 2 + NY) % NY
    two = send(mine, lambda y, c, x, z: ((y + 2) % NY, c, x, z))
    half = jnp.where(turn >= 2, two, mine)
    l0, w0, p10, l1, w1 = factor(core.astype(jnp.int32)[None], core_rows, other_rows)
    others, half, *_ = lax.optimization_barrier((others, half, l1, *own_quarters))

    upper = [send(others[N:], lambda y, c, x, z, d=d: (y, c, (x + d) % NX, z)) for d in (1, 2, 3)]
    lower = send(jnp.concatenate([q[:N] for q in own_quarters[1:]], 0), lambda y, c, x, z: (y, c, x, z ^ 1))
    one = send(half, lambda y, c, x, z: ((y + 1) % NY, c, x, z))
    info = jnp.stack([row_index, col_index, core == z % 2, z % 2, x]).astype(jnp.int32)
    first_part, turned = solve_own(info, w0, p10, w1, own_quarters)
    one, half, *_ = lax.optimization_barrier((one, half, first_part, lower, *upper))
    half = jnp.where(turn % 2 == 1, one, half)
    next_half = send(half, lambda y, c, x, z: (y, c, x, z ^ 1))
    rows = solve_rows(info, w0, w1, turned, first_part, others, lower, upper)
    next_half, rows = lax.optimization_barrier((next_half, rows))
    panel = jnp.stack([jnp.where(z % 2 == 0, half, next_half), jnp.where(z % 2 == 0, next_half, half)])
    other_panel = send(panel, lambda y, c, x, z: (y, 1 - c, x, z))

    out = update(info, flat_blocks.reshape(2, 4 * N * 4, 128), rows, panel, other_panel, l0, w0, p10, l1, w1)
    return out.reshape(matrix.shape)


def solution(mesh):
    return jax.shard_map(
        on_device,
        mesh=mesh,
        in_specs=(P(None, "row", None, None, "col", None),),
        out_specs=P(None, "row", None, None, "col", None),
        check_vma=False,
    )
```

```python
import jax
import jax.numpy as jnp
from jax import lax
from jax.experimental import pallas as pl
from jax.experimental.pallas import tpu as pltpu
from jax.sharding import PartitionSpec as P

F32 = jnp.float32
BF16 = jnp.bfloat16
N = 256
SLAB = 64
NY, NC, NX, NZ = 4, 2, 4, 8


def flat(y, c, x, z):
    return ((y * NC + c) * NX + x) * NZ + z


def pairs(fn):
    found = []
    for y in range(NY):
        for c in range(NC):
            for x in range(NX):
                for z in range(NZ):
                    to = fn(y, c, x, z)
                    if to is not None:
                        found.append((flat(y, c, x, z), flat(*to)))
    return found


def send(value, fn):
    return lax.ppermute(value, ("row", "col"), pairs(fn))


def sweep_slab(slab):
    left = [g[:, :128] for g in slab]
    right = [g[:, 128:] for g in slab]
    lane = lax.broadcasted_iota(jnp.int32, (8, 128), 1)
    sub = lax.broadcasted_iota(jnp.int32, (8, 128), 0)

    def splat(v):
        return jnp.broadcast_to(v, (8, 128))

    def assemble(rows):
        out = rows[0]
        for i in range(1, 8):
            out = jnp.where(sub == i, rows[i], out)
        return out

    z_left, z_right, u_left = [], [], []
    for s in range(len(slab)):
        a0, a1 = left[s], right[s]
        o = 8 * s
        cols = [splat(a0[:, o + j : o + j + 1]) for j in range(8)]
        d = [[splat(cols[j][i : i + 1, :]) for j in range(i + 1)] for i in range(8)]
        r0 = [splat(a0[i : i + 1, :]) for i in range(8)]
        r1 = [splat(a1[i : i + 1, :]) for i in range(8)]
        in_block = (lane >= o) & (lane < o + 8)
        r = []
        l = [[None] * 8 for _ in range(8)]
        zl, zr, ul = [], [], []
        for k in range(8):
            rk = lax.rsqrt(d[k][k])
            r.append(rk)
            for i in range(k + 1, 8):
                l[i][k] = d[i][k] * rk
            for j in range(k + 1, 8):
                for i in range(j, 8):
                    d[i][j] = d[i][j] - l[i][k] * l[j][k]
            x0 = jnp.where(in_block, jnp.where(lane == o + k, 1.0, 0.0).astype(F32), r0[k])
            x1 = r1[k]
            x2 = r0[k]
            for m in range(k):
                x0 = x0 - l[k][m] * zl[m]
                x1 = x1 - l[k][m] * zr[m]
                x2 = x2 - l[k][m] * ul[m]
            zl.append(x0 * rk)
            zr.append(x1 * rk)
            ul.append(x2 * rk)
        z_left.append(assemble(zl))
        z_right.append(assemble(zr))
        u_left.append(assemble(ul))
        for t in range(s + 1, len(slab)):
            coef = []
            for k in range(8):
                c = splat(left[t][:, o + k : o + k + 1])
                for m in range(k):
                    c = c - l[k][m] * coef[m]
                coef.append(c * r[k])
            x0 = jnp.where(in_block, 0.0, left[t])
            x1 = right[t]
            for k in range(8):
                x0 = x0 - coef[k] * zl[k]
                x1 = x1 - coef[k] * zr[k]
            left[t] = x0
            right[t] = x1
    return z_left, z_right, u_left


def factor_tile(m_ref, u_ref):
    row = lax.broadcasted_iota(jnp.int32, (N, N), 0)
    lan = lax.broadcasted_iota(jnp.int32, (N, N), 1)
    row_s = lax.broadcasted_iota(jnp.int32, (SLAB, N), 0)
    lan_s = lax.broadcasted_iota(jnp.int32, (SLAB, N), 1)

    @pl.loop(0, N // SLAB)
    def _(b):
        o = b * SLAB
        rows = pl.ds(pl.multiple_of(o, SLAB), SLAB)
        slab = pltpu.roll(m_ref[rows, :], N - o, 1)
        zl, zr, ul = sweep_slab([slab[8 * g : 8 * g + 8, :] for g in range(SLAB // 8)])
        zr = jnp.concatenate(zr, 0)
        z = jnp.concatenate([jnp.concatenate(zl, 0), zr], 1)
        u = jnp.concatenate([jnp.concatenate(ul, 0), zr], 1)
        z = jnp.where((lan_s < SLAB) & (lan_s > row_s), 0.0, z)
        z = pltpu.roll(z, o, 1)
        u = pltpu.roll(u, o, 1)
        u_ref[rows, :] = u

        @pl.when(b < N // SLAB - 1)
        def _():
            coef = jnp.where(lan_s >= o + SLAB, u, 0.0)
            update = lax.dot_general(
                coef, z, (((0,), (0,)), ((), ())), precision=lax.Precision.HIGHEST, preferred_element_type=F32
            )
            m = m_ref[...]
            m = jnp.where((row >= o + SLAB) & (lan >= o) & (lan < o + SLAB), 0.0, m)
            m_ref[...] = m - update

        m_ref[rows, :] = z


def dot_nt(a, b):
    return lax.dot_general(a, b, (((1,), (1,)), ((), ())), precision=lax.Precision.HIGHEST, preferred_element_type=F32)


def read_out(l_ref, w_ref, m_ref, u_ref):
    row = lax.broadcasted_iota(jnp.int32, (N, N), 0)
    lan = lax.broadcasted_iota(jnp.int32, (N, N), 1)
    l_ref[...] = jnp.where(row >= lan, u_ref[...].T, 0.0)
    w_ref[...] = jnp.where(row >= lan, m_ref[...], 0.0)


def factor_kernel(core_ref, own_ref, other_ref, l0_out, w0_out, p10_out, l1_out, w1_out, m_ref, u_ref, tiles, sem):
    l0_ref, w0_ref, p10_ref, l1_ref, w1_ref = (tiles.at[k] for k in range(5))
    outs = (l0_out, w0_out, p10_out, l1_out, w1_out)
    copies = [pltpu.make_async_copy(tiles.at[k], out, sem.at[k]) for k, out in enumerate(outs)]
    row = lax.broadcasted_iota(jnp.int32, (N, N), 0)
    lan = lax.broadcasted_iota(jnp.int32, (N, N), 1)

    def part(core, k, lo=0, hi=8):
        return jnp.where(core_ref[0] == core, own_ref[:, k, lo:hi, :], other_ref[:, k, lo:hi, :])

    def mirrored(core):
        t = jnp.concatenate([part(core, k).reshape(N, 128) for k in range(2)], 1)
        return jnp.where(row >= lan, t, t.T)

    def between():
        sides = [jnp.concatenate([part(core, 2, lo, lo + 4) for core in range(2)], 1) for lo in (0, 4)]
        return jnp.concatenate([side.reshape(N, 128) for side in sides], 1)

    m_ref[...] = mirrored(0)
    factor_tile(m_ref, u_ref)
    read_out(l0_ref, w0_ref, m_ref, u_ref)
    p10 = dot_nt(between(), w0_ref[...])
    p10_ref[...] = p10
    for copy in copies[:3]:
        copy.start()
    m_ref[...] = mirrored(1) - dot_nt(p10, p10)
    factor_tile(m_ref, u_ref)
    read_out(l1_ref, w1_ref, m_ref, u_ref)
    for copy in copies[3:]:
        copy.start()
    for copy in copies:
        copy.wait()


def factor(core, own, other):
    vmem = pl.BlockSpec(memory_space=pltpu.VMEM)
    return pl.pallas_call(
        factor_kernel,
        out_shape=[jax.ShapeDtypeStruct((N, N), F32)] * 5,
        in_specs=[pl.BlockSpec(memory_space=pltpu.SMEM), vmem, vmem],
        out_specs=[pl.BlockSpec(memory_space=pltpu.HBM)] * 5,
        scratch_shapes=[pltpu.VMEM((N, N), F32)] * 2 + [pltpu.VMEM((5, N, N), F32), pltpu.SemaphoreType.DMA((5,))],
        compiler_params=pltpu.CompilerParams(vmem_limit_bytes=60 << 20),
        cost_estimate=pl.CostEstimate(flops=10**9, bytes_accessed=60 << 20, transcendentals=0),
        name="factor",
    )(core, own, other)


def column_kernel(m_ref, *o_refs):
    for d, o_ref in enumerate(o_refs):
        @pl.when(pl.program_id(0) == d)
        def _(o_ref=o_ref):
            for half in range(2):
                o_ref[0, :, half * 128 : half * 128 + 128] = m_ref[pl.ds(half, N, stride=4), :]


def first_column(flat_blocks):
    out = lambda d: pl.BlockSpec((1, N, N), lambda k, h: (jnp.where(k == d, h, jnp.where(k < d, 0, 1)), 0, 0))
    return pl.pallas_call(
        column_kernel,
        grid=(4, 2),
        out_shape=[jax.ShapeDtypeStruct((2, N, N), F32)] * 4,
        in_specs=[pl.BlockSpec((4 * N, 128), lambda k, h: (k + 4 * h, 0))],
        out_specs=[out(d) for d in range(4)],
        compiler_params=pltpu.CompilerParams(
            vmem_limit_bytes=16 << 20, dimension_semantics=("arbitrary", "arbitrary")
        ),
        cost_estimate=pl.CostEstimate(flops=0, bytes_accessed=6 << 20, transcendentals=0),
        name="first_column",
    )(flat_blocks)


def order_kernel(slot_ref, *refs):
    pieces, o_ref = refs[:-1], refs[-1]
    for d, piece in enumerate(pieces):
        slot = lax.rem(slot_ref[0] + len(pieces) - d, len(pieces))
        o_ref[pl.ds(pl.multiple_of(slot * 128, 128), 128), :] = piece[...]


def order(slot, pieces):
    return pl.pallas_call(
        order_kernel,
        out_shape=jax.ShapeDtypeStruct((2 * N, N), F32),
        in_specs=[pl.BlockSpec(memory_space=pltpu.SMEM)] + [pl.BlockSpec(memory_space=pltpu.VMEM)] * 4,
        out_specs=pl.BlockSpec(memory_space=pltpu.VMEM),
        compiler_params=pltpu.CompilerParams(vmem_limit_bytes=8 << 20),
        cost_estimate=pl.CostEstimate(flops=0, bytes_accessed=1 << 20, transcendentals=0),
        name="order",
    )(slot, *pieces)


def split(v):
    hi = v.astype(BF16)
    return hi, (v - hi.astype(F32)).astype(BF16)


def split3(v):
    hi = v.astype(BF16)
    rest = v - hi.astype(F32)
    mid = rest.astype(BF16)
    return hi, mid, (rest - mid.astype(F32)).astype(BF16)


def six_left(v):
    hi, mid, lo = split3(v)
    return jnp.concatenate([lo, hi, mid, mid, hi, hi], 1)


def six_right(v):
    hi, mid, lo = split3(v)
    return jnp.concatenate([hi, lo, mid, hi, mid, hi], 0)


def dot16(a, b):
    return jnp.dot(a, b, preferred_element_type=F32)


def dot_nn(a, b):
    return jnp.dot(a, b, precision=lax.Precision.HIGHEST, preferred_element_type=F32)


def own_kernel(info_ref, w0_ref, p10_ref, w1_ref, a0, a1, a2, a3, o_ref, turned_ref, w_s):
    t = pl.program_id(0)

    @pl.when(t == 0)
    def _():
        turned_ref[...] = dot_nn(w1_ref[...], p10_ref[...])
        w_s[...] = six_right(jnp.where(info_ref[3] == 0, w0_ref[...], w1_ref[...]).T)

    for d, mine in enumerate((a0, a1, a2, a3)):
        @pl.when(t == d)
        def _(mine=mine):
            o_ref[0] = dot16(six_left(mine[...]), w_s[...])


def solve_own(info, w0, p10, w1, own_quarters):
    whole = lambda *shape: pl.BlockSpec(shape, lambda t: (0,) * len(shape))
    return pl.pallas_call(
        own_kernel,
        grid=(4,),
        in_specs=[pl.BlockSpec(memory_space=pltpu.SMEM)] + [whole(N, N)] * 3 + [whole(2 * N, N)] * 4,
        out_specs=[pl.BlockSpec((1, 2 * N, N), lambda t: (t, 0, 0)), whole(N, N)],
        out_shape=[jax.ShapeDtypeStruct((4, 2 * N, N), F32), jax.ShapeDtypeStruct((N, N), F32)],
        scratch_shapes=[pltpu.VMEM((6 * N, N), BF16)],
        compiler_params=pltpu.CompilerParams(vmem_limit_bytes=60 << 20, dimension_semantics=("arbitrary",)),
        cost_estimate=pl.CostEstimate(flops=2 * 10**9, bytes_accessed=60 << 20, transcendentals=0),
        name="solve_own",
    )(info, w0, p10, w1, *own_quarters)


def rows_kernel(info_ref, w0_ref, w1_ref, turned_ref, part_ref, others_ref, lower_ref, u1, u2, u3, o_ref, w_s, t_s):
    t = pl.program_id(0)
    even = info_ref[3] == 0

    @pl.when(t == 0)
    def _():
        w_s[...] = six_right(jnp.where(even, w1_ref[...], w0_ref[...]).T)
        t_s[...] = six_right(turned_ref[...].T)

    for d, upper in enumerate((None, u1, u2, u3)):
        @pl.when(t == d)
        def _(d=d, upper=upper):
            if d == 0:
                others = others_ref[...]
            else:
                others = jnp.concatenate([lower_ref[d * N - N : d * N, :], upper[...]], 0)
            part = part_ref[0]
            rest = dot16(six_left(others), w_s[...])
            first = jnp.where(even, part, rest)
            o_ref[0, :, :N] = first
            o_ref[0, :, N:] = jnp.where(even, rest, part) - dot16(six_left(first), t_s[...])


def solve_rows(info, w0, w1, turned, part, others, lower, upper):
    whole = lambda *shape: pl.BlockSpec(shape, lambda t: (0,) * len(shape))
    return pl.pallas_call(
        rows_kernel,
        grid=(4,),
        in_specs=[pl.BlockSpec(memory_space=pltpu.SMEM)]
        + [whole(N, N)] * 3
        + [pl.BlockSpec((1, 2 * N, N), lambda t: (t, 0, 0)), whole(2 * N, N), whole(3 * N, N)]
        + [whole(N, N)] * 3,
        out_specs=pl.BlockSpec((1, 2 * N, 2 * N), lambda t: (t, 0, 0)),
        out_shape=jax.ShapeDtypeStruct((4, 2 * N, 2 * N), F32),
        scratch_shapes=[pltpu.VMEM((6 * N, N), BF16)] * 2,
        compiler_params=pltpu.CompilerParams(vmem_limit_bytes=60 << 20, dimension_semantics=("arbitrary",)),
        cost_estimate=pl.CostEstimate(flops=5 * 10**9, bytes_accessed=9 << 20, transcendentals=0),
        name="solve_rows",
    )(info, w0, w1, turned, part, others, lower, *upper)


def update_kernel(
    info_ref, m_ref, p_ref, own_ref, other_ref, l0_ref, w0_ref, p10_ref, l1_ref, w1_ref, o_ref, x_s, right
):
    t = pl.program_id(0)
    p, q, keep_own, x = info_ref[0], info_ref[1], info_ref[2], info_ref[4]
    i = 8 * lax.rem(x - t + 4, 4) + p

    @pl.when(t == 0)
    def _():
        for value, kept in ((own_ref, 1), (other_ref, 0)):
            @pl.when(keep_own == kept)
            def _(value=value):
                x_s[...] = value[...]

        first = dot_nt(w0_ref[...], x_s[0])
        second = dot_nn(w1_ref[...], x_s[1].T - dot_nn(p10_ref[...], first))
        for k, panel in enumerate((first, second)):
            hi, lo = split(panel)
            for group, value in enumerate((hi, lo, hi)):
                at = 2 * N * group + N * k
                right[at : at + N, :] = value

    def put(h, b, value):
        for half in range(2):
            o_ref[h, pl.ds(2 * b + half, N, stride=4), :] = value[:, half * 128 : half * 128 + 128]

    def get(h, b):
        return jnp.concatenate([m_ref[h, pl.ds(2 * b + half, N, stride=4), :] for half in range(2)], 1)

    def change(h, b):
        hi, lo = split(p_ref[0, h * N : h * N + N, :])
        left = jnp.concatenate([lo, hi, hi], 1)
        product = dot16(left, right[:, b * N : b * N + N])
        put(h, b, get(h, b) - product)

    @pl.when(q > 1)
    def _():
        change(1, 0)

    @pl.when((q > 1) & (i >= q))
    def _():
        change(0, 0)

    @pl.when((q > 1) & (i < q) | (q == 1) & (i < 1))
    def _():
        put(0, 0, get(0, 0))

    @pl.when(i >= q)
    def _():
        change(1, 1)

    @pl.when(i < q)
    def _():
        put(1, 1, get(1, 1))

    put(0, 1, get(0, 1))

    for k, l_ref in enumerate((l0_ref, l1_ref)):
        cols = slice(k * N, k * N + N)

        @pl.when(q == k)
        def _(cols=cols):
            put(1, 0, p_ref[0, N:, cols])

        @pl.when((q == k) & (i > k))
        def _(cols=cols):
            put(0, 0, p_ref[0, :N, cols])

        @pl.when((q == k) & (i == k))
        def _(l_ref=l_ref):
            put(0, 0, l_ref[...])


def update(info, flat_blocks, rows, own, other, l0, w0, p10, l1, w1):
    whole = lambda *shape: pl.BlockSpec(shape, lambda t, info: (0,) * len(shape))
    tiles = pl.BlockSpec((2, 4 * N, 128), lambda t, info: (0, lax.rem(info[4] - t + 4, 4), 0))
    return pl.pallas_call(
        update_kernel,
        grid_spec=pltpu.PrefetchScalarGridSpec(
            num_scalar_prefetch=1,
            grid=(4,),
            in_specs=[tiles, pl.BlockSpec((1, 2 * N, 2 * N), lambda t, info: (t, 0, 0))]
            + [whole(2, 2 * N, N)] * 2
            + [whole(N, N)] * 5,
            out_specs=tiles,
            scratch_shapes=[pltpu.VMEM((2, 2 * N, N), F32)] + [pltpu.VMEM((6 * N, 2 * N), BF16)],
        ),
        out_shape=jax.ShapeDtypeStruct(flat_blocks.shape, F32),
        compiler_params=pltpu.CompilerParams(vmem_limit_bytes=40 << 20, dimension_semantics=("arbitrary",)),
        cost_estimate=pl.CostEstimate(flops=5 * 10**9, bytes_accessed=16 << 20, transcendentals=0),
        name="update",
    )(info, flat_blocks, rows, own, other, l0, w0, p10, l1, w1)


def after(value, *others):
    return lax.optimization_barrier((value, *others))[0]


def pick(index, options):
    out = options[0]
    for k in range(1, len(options)):
        out = jnp.where(index == k, options[k], out)
    return out


def on_device(matrix):
    row_index = lax.axis_index("row")
    col_index = lax.axis_index("col")
    y, core = row_index // NC, row_index % NC
    x, z = col_index // NZ, col_index % NZ
    flat_blocks = matrix.reshape(8 * N * 4, 128)
    column = first_column(flat_blocks)

    arrived = [
        send(column[d], lambda y, c, x, z, d=d: (y, c, d, z) if x == 0 and z < 2 else None) for d in (1, 2, 3)
    ]

    own_rows = lax.all_to_all(column[0][0].reshape(32, 8, N), "col", 0, 0, tiled=True)[:2]

    quarter = after(pick(x, [column[0], *arrived]), own_rows)

    parts = quarter.reshape(4, 128, N)
    sent = [
        send(
            lax.dynamic_index_in_dim(parts, (z // 2 + d) % 4, 0, keepdims=False),
            lambda y, c, x, z, d=d: (y, c, x, (z + 2 * d) % NZ) if z < 2 else None,
        )
        for d in (1, 2, 3)
    ]
    piece = pick(z // 2, [parts[0], *sent])
    tile_rows = after(own_rows, quarter)
    tile_rows = lax.all_to_all(jnp.broadcast_to(tile_rows[None], (8, 2, 8, N)), "row", 0, 0, tiled=True)
    lead, middle, last = tile_rows[0, 0], tile_rows[1, 0], tile_rows[1, 1]
    whole, part = jnp.where(core == 0, lead, last), jnp.where(core == 0, middle[:4], middle[4:])
    core_rows = jnp.stack([whole[:, :128], whole[:, 128:], jnp.concatenate([part[:, :128], part[:, 128:]], 0)])
    core_rows = lax.all_to_all(jnp.broadcast_to(core_rows[None], (32, 3, 8, 128)), "col", 0, 0, tiled=True)
    piece, core_rows = lax.optimization_barrier((piece, core_rows))
    pieces = [piece] + [send(piece, lambda y, c, x, z, d=d: (y, c, x, (z + 2 * d) % NZ)) for d in (1, 2, 3)]
    mine = order((z // 2).astype(jnp.int32)[None], pieces)
    other_rows = send(core_rows, lambda y, c, x, z: (y, 1 - c, x, z))
    mine, other_rows = lax.optimization_barrier((mine, other_rows))

    own_quarters = [mine] + [send(mine, lambda y, c, x, z, d=d: (y, c, (x + d) % NX, z)) for d in (1, 2, 3)]
    others = send(mine, lambda y, c, x, z: (y, c, x, z ^ 1))
    turn = (y - z // 2 + NY) % NY
    two = send(mine, lambda y, c, x, z: ((y + 2) % NY, c, x, z))
    half = jnp.where(turn >= 2, two, mine)
    l0, w0, p10, l1, w1 = factor(core.astype(jnp.int32)[None], core_rows, other_rows)
    others, half, *_ = lax.optimization_barrier((others, half, l1, *own_quarters))

    upper = [send(others[N:], lambda y, c, x, z, d=d: (y, c, (x + d) % NX, z)) for d in (1, 2, 3)]
    lower = send(jnp.concatenate([q[:N] for q in own_quarters[1:]], 0), lambda y, c, x, z: (y, c, x, z ^ 1))
    one = send(half, lambda y, c, x, z: ((y + 1) % NY, c, x, z))
    info = jnp.stack([row_index, col_index, core == z % 2, z % 2, x]).astype(jnp.int32)
    first_part, turned = solve_own(info, w0, p10, w1, own_quarters)
    one, half, *_ = lax.optimization_barrier((one, half, first_part, lower, *upper))
    half = jnp.where(turn % 2 == 1, one, half)
    next_half = send(half, lambda y, c, x, z: (y, c, x, z ^ 1))
    rows = solve_rows(info, w0, w1, turned, first_part, others, lower, upper)
    next_half, rows = lax.optimization_barrier((next_half, rows))
    panel = jnp.stack([jnp.where(z % 2 == 0, half, next_half), jnp.where(z % 2 == 0, next_half, half)])
    other_panel = send(panel, lambda y, c, x, z: (y, 1 - c, x, z))

    out = update(info, flat_blocks.reshape(2, 4 * N * 4, 128), rows, panel, other_panel, l0, w0, p10, l1, w1)
    return out.reshape(matrix.shape)


def solution(mesh):
    return jax.shard_map(
        on_device,
        mesh=mesh,
        in_specs=(P(None, "row", None, None, "col", None),),
        out_specs=P(None, "row", None, None, "col", None),
        check_vma=False,
    )
```
